512 devices in a mesh: lat: 128 (over y, z, x_hi), lon: 4 (over x_lo, core).
Axes of the slice: x: 4 (x_hi: 2, x_lo: 2; x = x_hi * 2 + x_lo), y: 4, z: 16, core: 2. Of those that a mesh axis runs over, the one named last changes fastest.
Arguments:
- fields: bfloat16 [2, 768, 48, 512], P(None, 'lat', 'lon'), may hold values from -24 to 24
- cotangent: bfloat16 [2, 768, 48, 512], P(None, 'lat', 'lon'), may hold values from -6 to 6
- norm_gain: float32 [512], replicated, may hold values from 0.1 to 1.9
- inner_weight: bfloat16 [512, 1536], replicated, may hold values from -0.25 to 0.25
- outer_weight: bfloat16 [512, 512], replicated, may hold values from -0.25 to 0.25
- bias_table: float32 [8, 759], replicated, may hold values from -4 to 256
- merge_gain: float32 [2048], replicated, may hold values from 0.1 to 1.9
- merge_weight: bfloat16 [2048, 1024], P('lat'), may hold values from -0.125 to 0.125
- split_weight: bfloat16 [1024, 2048], P('lat'), may hold values from -0.1875 to 0.1875
Outputs:
- outputs: bfloat16 [2, 768, 48, 512], P(None, 'lat', 'lon')
- grad_fields: bfloat16 [2, 768, 48, 512], P(None, 'lat', 'lon')
- grad_inner: float32 [512, 1536], P('lat', 'lon')
The draws below stay inside these ranges and needn't reach their ends.
All inputs are finite; a program needn't handle non-finite values.
Results may differ from the reference program's by a relative error of at most 0.0096.
Values may be sent and summed in bfloat16 or wider, within the bound.
A program may use at most 64 MiB of HBM per device.

```python
import math
import jax
import jax.numpy as jnp
from jax import lax

D = 512
HEADS = 8
HEAD_DIM = 64
LEVELS = 2
WIN_LAT = 6
WIN_LON = 12
NLAT = 768
NLON = 48
WIN = 144
RELS = 759
TOKENS = 73728


def draw_bias_table(key, part):
    key = jax.random.fold_in(key, 11)
    base_key = jax.random.fold_in(key, 0)
    table = jnp.clip(jax.random.normal(base_key, (HEADS, RELS), jnp.float32), -4.0, 4.0)
    return table


def spiked(values, stream_key, source, target, parts, factor):
    owner, partner = [(jnp.arange(values.shape[dim]) // (values.shape[dim] // parts)).reshape([-1 if axis == dim else 1 for axis in range(values.ndim)]) for dim in (source, target)]
    chosen = jax.random.permutation(stream_key, parts)[partner]
    strong = (owner == chosen) | (owner == (partner + parts // 2) % parts)
    return jnp.where(strong, factor * values, values)


def steps_of(own_key, extent, shards, least, high):
    level, own = 1.0, jax.random.fold_in(own_key, 6)
    for dim, parts in shards:
        draws = jnp.exp(jax.random.uniform(jax.random.fold_in(own, dim), (parts,), jnp.float32, least / len(shards), high / len(shards)))
        level = level * jnp.repeat(draws, extent[dim] // parts).reshape([-1 if axis == dim else 1 for axis in range(len(extent))])
    return level


def normal_values(own_key, extent, width, limit, cuts=(), kind=jnp.bfloat16):
    entries = width * jax.random.normal(own_key, extent, jnp.float32)
    if cuts:
        entries = entries * steps_of(own_key, extent, cuts, -0.22, 0.18)
    return jnp.clip(entries, -limit, limit).astype(kind)


def bell_draw_with(rng, shape, width, most, cuts, heavy, kind=jnp.bfloat16):
    values = width * jax.random.normal(rng, shape, jnp.float32)
    if cuts:
        values = values * steps_of(rng, shape, cuts, -0.22, 0.18)
    return jnp.clip(spiked(values, jax.random.fold_in(rng, 3), *heavy), -most, most).astype(kind)


def setup_inputs(seed: int = 0) -> dict:
    seeds = jax.random.split(jax.random.key(seed), 10)
    return {
        "fields": bell_draw_with(seeds[0], (LEVELS, NLAT, NLON, D), 1.0, 24.0, ((1, 128), (2, 4)), (1, 3, 128, 5.5)),
        "cotangent": normal_values(seeds[1], (LEVELS, NLAT, NLON, D), 1.0, 6.0, ((1, 128), (2, 4))),
        "norm_gain": jnp.clip(1.0 + 0.18 * jax.random.normal(seeds[2], (D,), jnp.float32), 0.1, 1.9),
        "inner_weight": normal_values(seeds[3], (D, 3 * D), D ** -0.5, 0.25),
        "outer_weight": normal_values(seeds[4], (D, D), D ** -0.5, 0.25),
        "bias_table": draw_bias_table(jax.random.fold_in(seeds[9], 71), 0),
        "merge_gain": jnp.clip(1.0 + 0.18 * jax.random.normal(seeds[6], (4 * D,), jnp.float32), 0.1, 1.9),
        "merge_weight": normal_values(seeds[7], (4 * D, 2 * D), (4 * D) ** -0.5, 0.125, ((0, 128),)),
        "split_weight": normal_values(seeds[8], (2 * D, 4 * D), (2 * D) ** -0.5, 0.1875, ((0, 128),)),
    }


def layer_norm(values, gain_vec):
    mean_of = lax.optimization_barrier(jnp.mean(values, axis=-1, keepdims=True))
    centred = values - mean_of
    variance = lax.optimization_barrier(jnp.mean(centred * centred, axis=-1, keepdims=True))
    return centred * lax.rsqrt(variance + 1e-05) * gain_vec

def relative_index():
    position = jnp.arange(WIN, dtype=jnp.int32)
    level_of = position // (WIN_LAT * WIN_LON)
    row_of = position // WIN_LON % WIN_LAT
    column = position % WIN_LON
    level_gap = level_of[:, None] - level_of[None, :] + LEVELS - 1
    row_gap = row_of[:, None] - row_of[None, :] + WIN_LAT - 1
    column_gap = column[:, None] - column[None, :] + WIN_LON - 1
    return ((level_gap * (2 * WIN_LAT - 1) + row_gap) * (2 * WIN_LON - 1) + column_gap).astype(jnp.int32)

def window_allowed(count_lat, count_lon, at_end):
    position = jnp.arange(WIN, dtype=jnp.int32)
    upper_half = position // WIN_LON % WIN_LAT >= WIN_LAT // 2
    window_row = jnp.arange(count_lat * count_lon, dtype=jnp.int32) // count_lon
    last_band = jnp.logical_and(window_row == count_lat - 1, at_end)
    group_of = jnp.logical_and(last_band[:, None], upper_half[None, :])
    return group_of[:, :, None] == group_of[:, None, :]

def to_windows(grid_in):
    levels, row_count, col_count, channels = grid_in.shape
    blocks = grid_in.reshape(levels, row_count // WIN_LAT, WIN_LAT, col_count // WIN_LON, WIN_LON, channels)
    return blocks.transpose(1, 3, 0, 2, 4, 5).reshape(-1, WIN, channels)

def from_windows(blocks, row_count, col_count):
    channels = blocks.shape[-1]
    grid_in = blocks.reshape(row_count // WIN_LAT, col_count // WIN_LON, LEVELS, WIN_LAT, WIN_LON, channels)
    return grid_in.transpose(2, 0, 3, 1, 4, 5).reshape(LEVELS, row_count, col_count, channels)

def to_pairs(grid_in):
    levels, row_count, col_count, channels = grid_in.shape
    blocks = grid_in.reshape(levels, row_count // 2, 2, col_count // 2, 2, channels)
    return blocks.transpose(0, 1, 3, 2, 4, 5).reshape(levels, row_count // 2, col_count // 2, 4 * channels)

def from_pairs(paired, channels):
    levels, half_rows, half_cols = (paired.shape[0], paired.shape[1], paired.shape[2])
    blocks = paired.reshape(levels, half_rows, half_cols, 2, 2, channels)
    return blocks.transpose(0, 1, 3, 2, 4, 5).reshape(levels, 2 * half_rows, 2 * half_cols, channels)

def attend(projected, pos_bias, allowed):
    blocks = projected.shape[0]
    heads = projected.astype(jnp.float32).reshape(blocks, WIN, 3, HEADS, HEAD_DIM)
    inv_root = HEAD_DIM ** (-0.5)
    scores = jnp.einsum('bqhe,bkhe->bhqk', heads[:, :, 0], heads[:, :, 1]) * inv_root + pos_bias[None]
    scores = jnp.where(allowed[:, None], scores, -1e+30)
    attention = jax.nn.softmax(scores, axis=-1)
    attention_b = lax.optimization_barrier(attention.astype(jnp.bfloat16))
    attended = jnp.einsum('bhqk,bkhe->bqhe', attention_b.astype(jnp.float32), heads[:, :, 2])
    return (attended.astype(jnp.bfloat16).reshape(blocks, WIN, D), attention, attention_b)

def attend_back(projected, attention, attention_b, grad_attended):
    blocks = projected.shape[0]
    heads = projected.astype(jnp.float32).reshape(blocks, WIN, 3, HEADS, HEAD_DIM)
    inv_root = HEAD_DIM ** (-0.5)
    grad_heads = grad_attended.astype(jnp.float32).reshape(blocks, WIN, HEADS, HEAD_DIM)
    grad_probs = jnp.einsum('bqhe,bkhe->bhqk', grad_heads, heads[:, :, 2])
    grad_values = jnp.einsum('bhqk,bqhe->bkhe', attention_b.astype(jnp.float32), grad_heads).astype(jnp.bfloat16)
    grad_scores = attention * (grad_probs - lax.optimization_barrier(jnp.sum(attention * grad_probs, axis=-1, keepdims=True)))
    grad_scores_b = lax.optimization_barrier(grad_scores.astype(jnp.bfloat16)).astype(jnp.float32)
    grad_query = (jnp.einsum('bhqk,bkhe->bqhe', grad_scores_b, heads[:, :, 1]) * inv_root).astype(jnp.bfloat16)
    grad_keys = (jnp.einsum('bhqk,bqhe->bkhe', grad_scores_b, heads[:, :, 0]) * inv_root).astype(jnp.bfloat16)
    return jnp.stack([grad_query, grad_keys, grad_values], axis=2).reshape(blocks, WIN, 3 * D)

def reference(fields, cotangent, norm_gain, inner_weight, outer_weight, bias_table, merge_gain, merge_weight, split_weight):
    half_lat = WIN_LAT // 2
    half_lon = WIN_LON // 2
    rolled = jnp.roll(fields, (-half_lat, -half_lon), axis=(1, 2))
    flat_rolled = rolled.reshape(-1, D).astype(jnp.float32)
    normed = layer_norm(flat_rolled, norm_gain).astype(jnp.bfloat16)
    projected = jnp.dot(normed, inner_weight, preferred_element_type=jnp.float32).astype(jnp.bfloat16)
    windows = to_windows(projected.reshape(LEVELS, NLAT, NLON, 3 * D))
    allowed = window_allowed(NLAT // WIN_LAT, NLON // WIN_LON, True)
    pos_bias = jnp.take(bias_table, relative_index(), axis=1)
    group_size = math.gcd(windows.shape[0], 8)
    grouped = windows.reshape(-1, group_size, WIN, 3 * D)
    allowed_groups = allowed.reshape(-1, group_size, WIN, WIN)

    def forward_group(item_set):
        return attend(item_set[0], pos_bias, item_set[1])[0]
    attended = lax.map(forward_group, (grouped, allowed_groups)).reshape(-1, WIN, D)
    attended = from_windows(attended, NLAT, NLON).reshape(-1, D)
    projected_out = jnp.dot(attended, outer_weight, preferred_element_type=jnp.float32)
    y_rolled = (flat_rolled + projected_out).astype(jnp.bfloat16).reshape(fields.shape)
    y_grid = jnp.roll(y_rolled, (half_lat, half_lon), axis=(1, 2))
    paired = to_pairs(y_grid)
    pair_shape = paired.shape
    pair_flat = paired.reshape(-1, 4 * D).astype(jnp.float32)
    merged_norm = layer_norm(pair_flat, merge_gain).astype(jnp.bfloat16)
    merged = jnp.dot(merged_norm, merge_weight, preferred_element_type=jnp.float32).astype(jnp.bfloat16)
    split_out = jnp.dot(merged, split_weight, preferred_element_type=jnp.float32)
    outputs = from_pairs((pair_flat + split_out).astype(jnp.bfloat16).reshape(pair_shape), D)
    grad_paired = to_pairs(cotangent).reshape(-1, 4 * D)
    grad_merged = jnp.dot(grad_paired, split_weight.T, preferred_element_type=jnp.float32).astype(jnp.bfloat16)
    grad_mnorm = jnp.dot(grad_merged, merge_weight.T, preferred_element_type=jnp.float32)
    _, merge_back = jax.vjp(lambda inputs: layer_norm(inputs, merge_gain), pair_flat)
    grad_y_pairs = (grad_paired.astype(jnp.float32) + merge_back(grad_mnorm)[0]).astype(jnp.bfloat16)
    grad_y = from_pairs(grad_y_pairs.reshape(pair_shape), D)
    grad_rolled_y = jnp.roll(grad_y, (-half_lat, -half_lon), axis=(1, 2))
    flat_grad = grad_rolled_y.reshape(-1, D)
    grad_attended = jnp.dot(flat_grad, outer_weight.T, preferred_element_type=jnp.float32).astype(jnp.bfloat16)
    grad_windows = to_windows(grad_attended.reshape(LEVELS, NLAT, NLON, D)).reshape(-1, group_size, WIN, D)

    def backward_group(item_set):
        unused, attention, attention_b = attend(item_set[0], pos_bias, item_set[1])
        return attend_back(item_set[0], attention, attention_b, item_set[2])
    grad_projected = lax.map(backward_group, (grouped, allowed_groups, grad_windows)).reshape(-1, WIN, 3 * D)
    grad_projected = from_windows(grad_projected, NLAT, NLON).reshape(-1, 3 * D)
    grad_normed = jnp.dot(grad_projected, inner_weight.T, preferred_element_type=jnp.float32)
    _, norm_back = jax.vjp(lambda inputs: layer_norm(inputs, norm_gain), flat_rolled)
    grad_rolled = (flat_grad.astype(jnp.float32) + norm_back(grad_normed)[0]).astype(jnp.bfloat16)
    grad_fields = jnp.roll(grad_rolled.reshape(fields.shape), (half_lat, half_lon), axis=(1, 2))
    grad_inner = jnp.dot(normed.T, grad_projected, preferred_element_type=jnp.float32) * (1.0 / math.sqrt(TOKENS))
    return (outputs, grad_fields, grad_inner)
```

```python
import functools
import math

import jax
import jax.numpy as jnp
import ml_dtypes
import numpy as np
from jax import lax
from jax.experimental import pallas as pl
from jax.experimental.pallas import tpu as pltpu
from jax.sharding import PartitionSpec as P

LEVELS = 2
WIN_LAT = 6
WIN_LON = 12
HEADS = 8
RELS = 759
SPAN = 384
QUAD = 48
ROWS = 4 * QUAD
WIN = 144
FAR = -1e30
Y, Z, XH = 4, 16, 2
MESH = pl.DeviceIdType.MESH
NT = (((1,), (1,)), ((), ()))
TN = (((0,), (0,)), ((), ()))
F32 = jnp.float32
BF16 = jnp.bfloat16


def dot(a, b, dims=(((1,), (0,)), ((), ()))):
    return lax.dot_general(a, b, dims, preferred_element_type=F32)


def orders():
    natural, quarter, pair = {}, {}, {}
    base, compact = {}, {}
    for l in range(LEVELS):
        for r in range(WIN_LAT):
            for c in range(WIN_LON):
                token = (l, r, c)
                natural[token] = (l * WIN_LAT + r) * 16 + c
                inside = (l * 3 + r % 3) * 6 + c % 6
                quarter[token] = ((r // 3) * 2 + c // 6) * QUAD + inside
                compact[token] = ((r // 3) * 2 + c // 6) * 36 + inside
                pair[token] = ((r % 2) * 2 + c % 2) * QUAD + (l * 3 + r // 2) * 6 + c // 2
                base[token] = (l * (2 * WIN_LAT - 1) + r) * (2 * WIN_LON - 1) + c
    to_quarter = np.zeros((ROWS, ROWS), ml_dtypes.bfloat16)
    to_pair = np.zeros((ROWS, ROWS), ml_dtypes.bfloat16)
    pair_of_quarter = np.zeros((ROWS, ROWS), ml_dtypes.bfloat16)
    dense = np.zeros((WIN, ROWS), ml_dtypes.bfloat16)
    pick = np.zeros((ROWS, SPAN), ml_dtypes.bfloat16)
    for token in natural:
        to_quarter[quarter[token], natural[token]] = 1
        to_pair[pair[token], natural[token]] = 1
        pair_of_quarter[pair[token], quarter[token]] = 1
        dense[compact[token], quarter[token]] = 1
        pick[quarter[token], base[token]] = 1
    return to_quarter, to_pair, pair_of_quarter, dense, pick


def bias_kernel(wrapped_ref, pick_ref, bias_ref):
    pick = pick_ref[...]
    used = jnp.sum(dot(jnp.ones((8, SPAN), BF16), pick, NT), axis=0, keepdims=True) > 0.5
    for h in range(HEADS):
        row = jnp.broadcast_to(wrapped_ref[h : h + 1, :], (SPAN, 2 * SPAN))
        shifted = pltpu.roll(row, 0, 1, stride=1, stride_axis=0)[:, :SPAN]
        high = shifted.astype(BF16)
        rest = shifted - high.astype(F32)
        middle = rest.astype(BF16)
        low = (rest - middle.astype(F32)).astype(BF16)
        total = jnp.zeros((ROWS, ROWS), F32)
        for part in (low, middle, high):
            total = total + dot(dot(pick, part).astype(BF16), pick, NT)
        bias_ref[h] = jnp.where(used, total, FAR)


def norm_parts(values):
    mean = jnp.mean(values, axis=-1, keepdims=True)
    centred = values - mean
    variance = jnp.mean(centred * centred, axis=-1, keepdims=True)
    scale = lax.rsqrt(variance + 1e-05)
    return centred * scale, scale


def norm_back(unit, scale, grad, gain):
    g = grad * gain
    middle = jnp.mean(g, axis=-1, keepdims=True)
    along = jnp.mean(g * unit, axis=-1, keepdims=True)
    return scale * (g - middle - unit * along)


def main_kernel(
    lon_size,
    fields, cotangent, gain, inner, outer, bias, merge_gain, merge_shard, split_shard,
    to_quarter, to_pair, pair_of_quarter, dense,
    outputs, grad_fields, grad_inner,
    nat, quads, win, cot_all, norm_all, raw, stack, split_w, merge_w,
    y_out, y_in, gm_out, gm_in, gy_out, gy_in, gf_out, gf_in, att, proj, normed,
    toks_all, gp, gp_out, gp_in, dw_out, dw_in, z_out, z_in, so_out, so_in, unit_keep,
    ssem, rsem, zsend, zrecv,
):
    D = fields.shape[-1]
    MS = D // 2
    CW = 3 * D // lon_size
    KB = 8
    HD2 = 2 * D // HEADS
    i, j = lax.axis_index("lat"), lax.axis_index("lon")
    lat_size = Y * Z * XH
    xh = lax.rem(i, XH)
    z = lax.rem(i // XH, Z)
    y = i // (XH * Z)

    def at(yy, zz, xx):
        return (yy * Z + zz) * XH + xx

    def lat_by(d):
        return lax.rem(i + d + lat_size, lat_size)

    def lon_by(d):
        return lax.rem(j + d + lon_size, lon_size)

    def y_by(d):
        return lax.rem(y + d + Y, Y)

    def z_by(d):
        return lax.rem(z + d, Z)

    sems = iter(range(ssem.shape[0]))
    sent = []

    def push(src, dst, lat, lon):
        k = next(sems)
        copy = pltpu.make_async_remote_copy(
            src_ref=src, dst_ref=dst, send_sem=ssem.at[k], recv_sem=rsem.at[k],
            device_id=(lat, lon), device_id_type=MESH,
        )
        copy.start()
        sent.append(copy)
        return copy

    def arrive(copies):
        for copy in copies:
            copy.wait_recv()

    def to_natural(src):
        nat[...] = jnp.zeros((ROWS, D), BF16)
        for l in range(LEVELS):
            for r in range(WIN_LAT):
                start = (l * WIN_LAT + r) * 16
                nat[start : start + WIN_LON, :] = src[l, r]
        return nat[...]

    quads[...] = dot(to_quarter[...], to_natural(fields)).astype(BF16).reshape(4, QUAD, D)
    win[0] = quads[3]

    for k in range(KB):
        stack[8 * k : 8 * k + 8, :] = split_shard[:, MS * k : MS * (k + 1)].astype(F32)
    row = lax.broadcasted_iota(jnp.int32, (16, 64), 0)
    col = lax.broadcasted_iota(jnp.int32, (16, 64), 1)
    sel = (col == (row // 2) * 8 + 2 * j + row % 2).astype(F32).astype(BF16)
    raw[z] = dot(sel, stack[...].astype(BF16)).astype(BF16)
    own = lax.broadcasted_iota(jnp.int32, (2 * D, MS), 1)
    place = ((own // (2 * Z * XH)) * Z + (own // 2) % Z) * XH + (own // (2 * Z)) % XH
    col = lax.broadcasted_iota(jnp.int32, (2 * D, MS), 0)
    sel = (col == 8 * place + 2 * j + own % 2).astype(F32).astype(BF16)
    merge_w[y, z, xh] = dot(merge_shard[...], sel).astype(BF16)

    partners = []
    for a, b in ((0, 1), (1, 0), (1, 1)):
        partners += [(lat_by(a), lon_by(b)), (lat_by(-a), lon_by(-b))]
    for d in range(1, lon_size):
        partners.append((i, lon_by(d)))
    plane = [(dy, dx) for dy in range(Y) for dx in range(XH) if dy or dx]
    for dy, dx in plane:
        partners.append((at(y_by(dy), z, lax.rem(xh + dx, XH)), j))
    barrier = pltpu.get_barrier_semaphore()
    for lat, lon in partners:
        pl.semaphore_signal(barrier, inc=1, device_id=(lat, lon), device_id_type=MESH)

    @pl.loop(1, Z)
    def _(d):
        pl.semaphore_signal(
            barrier, inc=1, device_id=(at(y, z_by(d), xh), j), device_id_type=MESH
        )

    pl.semaphore_wait(barrier, len(partners) + Z - 1)

    def roll_in(src, dst):
        return [
            push(src.at[(1 - a) * 2 + 1 - b], dst.at[a * 2 + b], lat_by(-a), lon_by(-b))
            for a, b in ((0, 1), (1, 0), (1, 1))
        ]

    def roll_out(src, dst):
        return [
            push(src.at[a * 2 + b], dst.at[(1 - a) * 2 + 1 - b], lat_by(a), lon_by(b))
            for a, b in ((0, 1), (1, 0), (1, 1))
        ]

    def z_copy(kind, d, src, dst):
        return pltpu.make_async_remote_copy(
            src_ref=src, dst_ref=dst, send_sem=zsend.at[kind, d], recv_sem=zrecv.at[kind, d],
            device_id=(at(y, z_by(d), xh), j), device_id_type=MESH,
        )

    def split_z(d):
        return z_copy(0, d, raw.at[z], raw.at[z])

    def merge_z(d):
        return z_copy(1, d, merge_w.at[y, z, xh], merge_w.at[y, z, xh])

    def sums_z(d):
        return z_copy(2, d, z_out.at[z_by(d)], z_in.at[z])

    def z_start(make):
        @pl.loop(1, Z)
        def _(d):
            make(d).start()

    def z_arrive(make):
        @pl.loop(1, Z)
        def _(d):
            make(d).wait_recv()

    fields_move = roll_in(quads, win)
    z_start(split_z)
    z_start(merge_z)

    def lanes(rows):
        return jnp.concatenate([rows[QUAD * s : QUAD * (s + 1)] for s in range(4)], axis=1)

    def stacked(wide):
        return jnp.concatenate([wide[:, D * s : D * (s + 1)] for s in range(4)], axis=0)

    cot_all[j] = lanes(dot(to_pair[...], to_natural(cotangent)).astype(BF16))
    cot_move = [push(cot_all.at[j], cot_all.at[j], i, lon_by(d)) for d in range(1, lon_size)]

    arrive(fields_move)
    rolled = win[...].reshape(ROWS, D).astype(F32)
    unit, scale = norm_parts(rolled)
    unit_keep[...] = unit
    normed[...] = (unit * gain[...]).astype(BF16)
    proj[...] = dot(normed[...], inner[...]).astype(BF16)

    z_arrive(split_z)
    full = Z * 16
    out = lax.broadcasted_iota(jnp.int32, (full, full), 0)
    src = lax.broadcasted_iota(jnp.int32, (full, full), 1)
    want = ((out % (2 * Z)) // 2) * 16 + (out // (2 * Z)) * 2 + out % 2
    regroup = (src == want).astype(F32).astype(BF16)
    split_w[y, xh] = dot(regroup, raw[...].reshape(full, MS)).astype(BF16).reshape(KB, 2 * Z, MS)
    other = lax.rem(xh + 1, XH)
    split_x = push(split_w.at[y, xh], split_w.at[y, xh], at(y, z, other), j)

    half_q = lax.broadcasted_iota(jnp.int32, (ROWS, ROWS), 0) // (2 * QUAD)
    half_k = lax.broadcasted_iota(jnp.int32, (ROWS, ROWS), 1) // (2 * QUAD)
    allowed = jnp.logical_or(half_q == half_k, i != lat_size - 1)
    first = lax.broadcasted_iota(jnp.int32, (ROWS, HD2), 1) < HD2 // 2
    inv_root = (HD2 // 2) ** -0.5

    def of_head(values, h):
        return jnp.where(first if h % 2 == 0 else jnp.logical_not(first), values, jnp.zeros_like(values))

    def attend(pair):
        at_q = slice(HD2 * pair, HD2 * (pair + 1))
        at_k = slice(D + HD2 * pair, D + HD2 * (pair + 1))
        at_v = slice(2 * D + HD2 * pair, 2 * D + HD2 * (pair + 1))
        q, k, v = proj[:, at_q], proj[:, at_k], proj[:, at_v]
        results = []
        for h in (2 * pair, 2 * pair + 1):
            scores = dot(of_head(q, h), k, NT) * inv_root + bias[h]
            scores = jnp.where(allowed, scores, FAR)
            weights = jnp.exp(scores - jnp.max(scores, axis=-1, keepdims=True))
            weights = weights / jnp.sum(weights, axis=-1, keepdims=True)
            att[h] = weights
            results.append(dot(weights.astype(BF16), v))
        return jnp.where(first, results[0], results[1]).astype(BF16)

    attended = [attend(0), attend(1)]

    z_arrive(merge_z)
    merge_x = push(merge_w.at[y, :, xh], merge_w.at[y, :, xh], at(y, z, other), j)
    arrive([split_x])

    def y_spread(whole):
        return [push(whole.at[y], whole.at[y], at(y_by(d), z, xh), j) for d in (1, -1)]

    split_y = y_spread(split_w)

    attended += [attend(2), attend(3)]
    attended = jnp.concatenate(attended, axis=1)
    y_rolled = (rolled + dot(attended, outer[...])).astype(BF16)
    y_out[...] = y_rolled.reshape(4, QUAD, D)
    y_in[3] = y_out[0]
    y_move = roll_out(y_out, y_in)

    arrive([merge_x])
    merge_y = y_spread(merge_w)

    row = lax.broadcasted_iota(jnp.int32, (D, D), 0)
    col = lax.broadcasted_iota(jnp.int32, (D, D), 1)
    block = col // (4 * Z)
    want = ((block // XH) * Z + (col // 4) % Z) * (4 * XH) + (block % XH) * 4 + col % 4
    swap = (row == want).astype(F32).astype(BF16)
    toks = dot(dense[...], normed[...]).astype(BF16)
    toks_all[j] = dot(toks, swap).astype(BF16)
    toks_move = [push(toks_all.at[j], toks_all.at[j], i, lon_by(d)) for d in range(1, lon_size)]

    arrive(y_move)
    y_pairs = lanes(dot(pair_of_quarter[...], y_in[...].reshape(ROWS, D)))
    pair_unit, pair_scale = norm_parts(y_pairs)
    norm_all[j] = (pair_unit * merge_gain[...]).astype(BF16)
    norm_move = [push(norm_all.at[j], norm_all.at[j], i, lon_by(d)) for d in range(1, lon_size)]

    def y_forward(whole, halves):
        return [
            push(halves(whole, y_by(-1), 0), halves(whole, y_by(-1), 0), at(y_by(1), z, xh), j),
            push(halves(whole, y_by(1), 1), halves(whole, y_by(1), 1), at(y_by(-1), z, xh), j),
        ]

    arrive(split_y)
    split_f = y_forward(split_w, lambda w, yy, part: w.at[yy, part])
    arrive(merge_y)
    merge_f = y_forward(merge_w, lambda w, yy, part: w.at[yy, pl.ds(part * (Z // 2), Z // 2)])

    arrive(cot_move)
    arrive(split_f)

    def split_block(k):
        return split_w[:, :, k].reshape(MS, MS)

    cots = cot_all[...].reshape(lon_size * QUAD, 4 * D)
    grad_merged = dot(cots[:, :MS], split_block(0), NT)
    for k in range(1, KB):
        grad_merged = grad_merged + dot(cots[:, MS * k : MS * (k + 1)], split_block(k), NT)
    grad_merged = grad_merged.astype(BF16)
    arrive(merge_f)
    merge_full = merge_w[...].reshape(4 * D, MS)
    gm_out[...] = dot(grad_merged, merge_full, NT).astype(BF16).reshape(lon_size, QUAD, 4 * D)

    def scatter(src, dst):
        return [push(src.at[lon_by(d)], dst.at[j], i, lon_by(d)) for d in range(1, lon_size)]

    def total(mine, received):
        result = mine[j].astype(F32)
        for d in range(1, lon_size):
            result = result + received[lon_by(-d)].astype(F32)
        return result

    gm_move = scatter(gm_out, gm_in)

    arrive(norm_move)
    merged = dot(norm_all[...].reshape(lon_size * QUAD, 4 * D), merge_full).astype(BF16)
    for k in range(KB):
        part = dot(merged, split_block(k)).astype(BF16)
        so_out[:, :, MS * k : MS * (k + 1)] = part.reshape(lon_size, QUAD, MS)

    arrive(gm_move)
    grad_mnorm = total(gm_out, gm_in)
    grad_y = cot_all[j].astype(F32) + norm_back(pair_unit, pair_scale, grad_mnorm, merge_gain[...])
    grad_y = dot(pair_of_quarter[...], stacked(grad_y.astype(BF16)), TN).astype(BF16)
    gy_out[...] = grad_y.reshape(4, QUAD, D)
    gy_in[0] = gy_out[3]
    gy_move = roll_in(gy_out, gy_in)
    so_move = scatter(so_out, so_in)

    arrive(gy_move)
    grad_rolled_y = gy_in[...].reshape(ROWS, D)
    grad_attended = dot(grad_rolled_y, outer[...], NT).astype(BF16)
    for pair in range(HEADS // 2):
        at_q = slice(HD2 * pair, HD2 * (pair + 1))
        at_k = slice(D + HD2 * pair, D + HD2 * (pair + 1))
        at_v = slice(2 * D + HD2 * pair, 2 * D + HD2 * (pair + 1))
        q, k, v = proj[:, at_q], proj[:, at_k], proj[:, at_v]
        g = grad_attended[:, at_q]
        found = []
        for h in (2 * pair, 2 * pair + 1):
            weights = att[h]
            grad_p = dot(of_head(g, h), v, NT)
            grad_v = dot(weights.astype(BF16), g, TN)
            shared = jnp.sum(weights * grad_p, axis=-1, keepdims=True)
            grad_s = (weights * (grad_p - shared)).astype(BF16)
            found.append((dot(grad_s, k) * inv_root, dot(grad_s, q, TN) * inv_root, grad_v))
        for where, even, odd in zip((at_q, at_k, at_v), *found):
            gp[:, where] = jnp.where(first, even, odd).astype(BF16)
    few = dot(dense[...], gp[...]).astype(BF16)
    for d in range(lon_size):
        gp_out[d] = few[:, CW * d : CW * (d + 1)]
    gp_move = scatter(gp_out, gp_in)
    gp_in[j] = gp_out[j]

    grad_normed = dot(gp[...], inner[...], NT)
    grad_in = grad_rolled_y.astype(F32) + norm_back(unit_keep[...], scale, grad_normed, gain[...])
    gf_out[...] = grad_in.astype(BF16).reshape(4, QUAD, D)
    gf_in[3] = gf_out[0]
    gf_move = roll_out(gf_out, gf_in)

    arrive(toks_move)
    arrive(gp_move)
    tokens = lon_size * WIN
    summed = dot(toks_all[...].reshape(tokens, D), gp_in[...].reshape(tokens, CW), TN)
    dw_out[...] = summed.astype(BF16).reshape(Y * XH, 4 * Z, CW)
    dw_move = []
    for dy, dx in plane:
        yy, xx = y_by(dy), lax.rem(xh + dx, XH)
        dw_move.append(push(dw_out.at[yy * XH + xx], dw_in.at[y * XH + xh], at(yy, z, xx), j))

    def from_pairs(wide):
        return dot(to_pair[...], stacked(wide), TN).astype(BF16)

    def put(dst, rows):
        for l in range(LEVELS):
            for r in range(WIN_LAT):
                start = (l * WIN_LAT + r) * 16
                dst[l, r] = rows[start : start + WIN_LON]

    arrive(so_move)
    put(outputs, from_pairs((y_pairs + total(so_out, so_in)).astype(BF16)))

    arrive(dw_move)
    mine = dw_out[y * XH + xh].astype(F32)
    for dy, dx in plane:
        slot = y_by(-dy) * XH + lax.rem(xh + dx, XH)
        mine = mine + dw_in[slot].astype(F32)
    mine = mine.astype(BF16)
    CB = CW // 3
    tall = jnp.concatenate([mine[:, CB * c : CB * (c + 1)] for c in range(3)], axis=0)
    row = lax.broadcasted_iota(jnp.int32, (16 * Z, 12 * Z), 0)
    col = lax.broadcasted_iota(jnp.int32, (16 * Z, 12 * Z), 1)
    inner_row = row % 16
    want = (inner_row // 4) * (4 * Z) + (row // 16) * 4 + inner_row % 4
    spread = jnp.logical_and(col == want, inner_row < 12).astype(F32).astype(BF16)
    z_out[...] = dot(spread, tall).astype(BF16).reshape(Z, 16, CB)
    z_start(sums_z)
    z_in[z] = z_out[z]

    arrive(gf_move)
    put(grad_fields, dot(to_quarter[...], gf_in[...].reshape(ROWS, D), TN).astype(BF16))

    z_arrive(sums_z)
    owned = jnp.sum(z_in[...].astype(F32), axis=0)
    shrink = 1.0 / math.sqrt(WIN * lat_size * lon_size)
    for c in range(3):
        grad_inner[:, CB * c : CB * (c + 1)] = owned[4 * c : 4 * c + 4] * shrink

    for copy in sent:
        copy.wait_send()

    @pl.loop(1, Z)
    def _(d):
        split_z(d).wait_send()
        merge_z(d).wait_send()
        sums_z(d).wait_send()


def local(
    lon_size, fields, cotangent, norm_gain, inner_weight, outer_weight, bias_table, merge_gain,
    merge_weight, split_weight,
):
    D = fields.shape[-1]
    to_quarter, to_pair, pair_of_quarter, dense, pick = (jnp.asarray(a) for a in orders())
    middle = (RELS - 1) // 2
    wrapped = jnp.concatenate(
        [
            bias_table[:, middle::-1],
            jnp.zeros((HEADS, 2 * SPAN - RELS), F32),
            bias_table[:, :middle:-1],
        ],
        axis=1,
    )
    vmem = pl.BlockSpec(memory_space=pltpu.VMEM)
    bias = pl.pallas_call(
        bias_kernel,
        out_shape=jax.ShapeDtypeStruct((HEADS, ROWS, ROWS), F32),
        in_specs=[vmem] * 2,
        out_specs=vmem,
        compiler_params=pltpu.CompilerParams(vmem_limit_bytes=32 * 1024 * 1024),
    )(wrapped, pick)
    MS, CW = D // 2, 3 * D // lon_size

    def buf(*shape, dtype=BF16):
        return pltpu.VMEM(shape, dtype)

    quarters = (4, QUAD, D)
    wide = (lon_size, QUAD, 4 * D)
    scratch = [
        buf(ROWS, D), buf(*quarters), buf(*quarters), buf(*wide), buf(*wide),
        buf(Z, 16, MS), buf(64, MS, dtype=F32), buf(Y, XH, 8, 2 * Z, MS), buf(Y, Z, XH, 16, MS),
        buf(*quarters), buf(*quarters), buf(*wide), buf(*wide), buf(*quarters), buf(*quarters),
        buf(*quarters), buf(*quarters), buf(HEADS, ROWS, ROWS, dtype=F32), buf(ROWS, 3 * D),
        buf(ROWS, D),
        buf(lon_size, WIN, D), buf(ROWS, 3 * D), buf(lon_size, WIN, CW), buf(lon_size, WIN, CW),
        buf(Y * XH, 4 * Z, CW), buf(Y * XH, 4 * Z, CW), buf(Z, 16, CW // 3), buf(Z, 16, CW // 3),
        buf(*wide), buf(*wide), buf(ROWS, D, dtype=F32),
    ]
    count = 4 * 3 + 6 * (lon_size - 1) + 2 * 5 + (Y * XH - 1)
    scratch += [
        pltpu.SemaphoreType.DMA((count,)), pltpu.SemaphoreType.DMA((count,)),
        pltpu.SemaphoreType.DMA((3, Z)), pltpu.SemaphoreType.DMA((3, Z)),
    ]
    return pl.pallas_call(
        functools.partial(main_kernel, lon_size),
        out_shape=(
            jax.ShapeDtypeStruct(fields.shape, BF16),
            jax.ShapeDtypeStruct(fields.shape, BF16),
            jax.ShapeDtypeStruct((4, CW), F32),
        ),
        in_specs=[vmem] * 13,
        out_specs=(vmem,) * 3,
        scratch_shapes=scratch,
        compiler_params=pltpu.CompilerParams(
            collective_id=0, has_side_effects=True, vmem_limit_bytes=48 * 1024 * 1024
        ),
    )(
        fields, cotangent, norm_gain.reshape(1, D), inner_weight, outer_weight, bias,
        merge_gain.reshape(1, 4 * D), merge_weight, split_weight,
        to_quarter, to_pair, pair_of_quarter, dense,
    )


def solution(mesh):
    return jax.shard_map(
        functools.partial(local, mesh.shape["lon"]),
        mesh=mesh,
        in_specs=(
            P(None, "lat", "lon", None),
            P(None, "lat", "lon", None),
            P(),
            P(),
            P(),
            P(),
            P(),
            P("lat", None),
            P("lat", None),
        ),
        out_specs=(P(None, "lat", "lon", None), P(None, "lat", "lon", None), P("lat", "lon")),
        check_vma=False,
    )
```

```python
import functools
import math

import jax
import jax.numpy as jnp
import ml_dtypes
import numpy as np
from jax import lax
from jax.experimental import pallas as pl
from jax.experimental.pallas import tpu as pltpu
from jax.sharding import PartitionSpec as P

LEVELS = 2
WIN_LAT = 6
WIN_LON = 12
HEADS = 8
RELS = 759
SPAN = 384
QUAD = 48
ROWS = 4 * QUAD
WIN = 144
FAR = -1e30
Y, Z, XH = 4, 16, 2
MESH = pl.DeviceIdType.MESH
NT = (((1,), (1,)), ((), ()))
TN = (((0,), (0,)), ((), ()))
F32 = jnp.float32
BF16 = jnp.bfloat16


def dot(a, b, dims=(((1,), (0,)), ((), ()))):
    return lax.dot_general(a, b, dims, preferred_element_type=F32)


def orders():
    natural, quarter, pair = {}, {}, {}
    base, compact = {}, {}
    for l in range(LEVELS):
        for r in range(WIN_LAT):
            for c in range(WIN_LON):
                token = (l, r, c)
                natural[token] = (r * WIN_LON + c) * LEVELS + l
                inside = (l * 3 + r % 3) * 6 + c % 6
                quarter[token] = ((r // 3) * 2 + c // 6) * QUAD + inside
                compact[token] = ((r // 3) * 2 + c // 6) * 36 + inside
                pair[token] = ((r % 2) * 2 + c % 2) * QUAD + (l * 3 + r // 2) * 6 + c // 2
                base[token] = (l * (2 * WIN_LAT - 1) + r) * (2 * WIN_LON - 1) + c
    to_quarter = np.zeros((ROWS, WIN), ml_dtypes.bfloat16)
    to_pair = np.zeros((ROWS, WIN), ml_dtypes.bfloat16)
    pair_of_quarter = np.zeros((ROWS, ROWS), ml_dtypes.bfloat16)
    dense = np.zeros((WIN, ROWS), ml_dtypes.bfloat16)
    pick = np.zeros((ROWS, SPAN), ml_dtypes.bfloat16)
    for token in natural:
        to_quarter[quarter[token], natural[token]] = 1
        to_pair[pair[token], natural[token]] = 1
        pair_of_quarter[pair[token], quarter[token]] = 1
        dense[compact[token], quarter[token]] = 1
        pick[quarter[token], base[token]] = 1
    return to_quarter, to_pair, pair_of_quarter, dense, pick


def make_bias(table_ref, padded_ref, pick, bias_ref):
    middle = (RELS - 1) // 2
    padded_ref[...] = jnp.zeros((HEADS, 2 * SPAN), F32)
    padded_ref[:, :RELS] = table_ref[...]
    back = 2 * SPAN - middle
    padded_ref[...] = pltpu.roll(padded_ref[...], back % 128, 1)
    used = jnp.sum(dot(jnp.ones((8, SPAN), BF16), pick, NT), axis=0, keepdims=True) > 0.5
    for h in range(HEADS):
        row = jnp.broadcast_to(padded_ref[h : h + 1, :], (SPAN, 2 * SPAN))
        shifted = pltpu.roll(row, back // 128 * 128, 1, stride=1, stride_axis=0)[:, :SPAN]
        high = shifted.astype(BF16)
        rest = shifted - high.astype(F32)
        middle_part = rest.astype(BF16)
        low = (rest - middle_part.astype(F32)).astype(BF16)
        total = jnp.zeros((ROWS, ROWS), F32)
        for part in (low, middle_part, high):
            total = total + dot(dot(pick, part, NT).astype(BF16), pick, NT)
        bias_ref[h] = jnp.where(used, total, FAR)


def norm_parts(values):
    mean = jnp.mean(values, axis=-1, keepdims=True)
    centred = values - mean
    variance = jnp.mean(centred * centred, axis=-1, keepdims=True)
    scale = lax.rsqrt(variance + 1e-05)
    return centred * scale, scale


def norm_back(unit, scale, grad, gain):
    g = grad * gain
    middle = jnp.mean(g, axis=-1, keepdims=True)
    along = jnp.mean(g * unit, axis=-1, keepdims=True)
    return scale * (g - middle - unit * along)


def main_kernel(
    lon_size,
    *refs,
):
    operands, refs = refs[:14], refs[14:]
    (
        outputs, grad_fields, grad_inner,
        nat, quads, win, cot_all, norm_all, raw, stack, split_w, merge_w,
        y_out, y_in, gm_out, gy_out, gy_in, gf_out, gf_in, att, proj, normed,
        toks_all, gp, gp_out, gp_in, dw_out, dw_in, z_out, z_in, so_out, unit_keep,
        bias, padded, gp_mid, gm_mid, so_mid, cross_out, cross_in,
        ssem, rsem, zsend, zrecv, lsem,
        *local_refs,
    ) = refs
    loads = [
        pltpu.make_async_copy(src, dst, lsem.at[k])
        for k, (src, dst) in enumerate(zip(operands, local_refs))
    ]
    for load in loads:
        load.start()
    (
        fields, to_quarter, split_shard, merge_shard, cotangent, to_pair, gain, inner, table,
        pick, outer, pair_of_quarter, merge_gain, dense,
    ) = local_refs
    loads = dict(zip(map(id, local_refs), loads))

    def ready(*wanted):
        for ref in wanted:
            loads[id(ref)].wait()

    D = fields.shape[-1]
    MS = D // 2
    CW = 3 * D // lon_size
    KB = 8
    HD2 = 2 * D // HEADS
    i, j = lax.axis_index("lat"), lax.axis_index("lon")
    lat_size = Y * Z * XH
    xh = lax.rem(i, XH)
    z = lax.rem(i // XH, Z)
    y = i // (XH * Z)
    other = lax.rem(xh + 1, XH)
    mate = j + 1 - 2 * lax.rem(j, 2)
    across = lax.rem(j + 2, lon_size)
    beyond = lax.rem(mate + 2, lon_size)

    def at(yy, zz, xx):
        return (yy * Z + zz) * XH + xx

    def lat_by(d):
        return lax.rem(i + d + lat_size, lat_size)

    def lon_by(d):
        return lax.rem(j + d + lon_size, lon_size)

    def y_by(d):
        return lax.rem(y + d + Y, Y)

    def z_by(d):
        return lax.rem(z + d, Z)

    sems = iter(range(ssem.shape[0]))
    sent = []

    def push(src, dst, lat, lon):
        k = next(sems)
        copy = pltpu.make_async_remote_copy(
            src_ref=src, dst_ref=dst, send_sem=ssem.at[k], recv_sem=rsem.at[k],
            device_id=(lat, lon), device_id_type=MESH,
        )
        copy.start()
        sent.append(copy)
        return copy

    def arrive(copies):
        for copy in copies:
            copy.wait_recv()

    partners = []
    for a, b in ((0, 1), (1, 0), (1, 1)):
        partners += [(lat_by(a), lon_by(b)), (lat_by(-a), lon_by(-b))]
    for d in range(1, lon_size):
        partners.append((i, lon_by(d)))
    plane = [(dy, dx) for dy in range(Y) for dx in range(XH) if dy or dx]
    for dy, dx in plane:
        partners.append((at(y_by(dy), z, lax.rem(xh + dx, XH)), j))
    barrier = pltpu.get_barrier_semaphore()
    for lat, lon in partners:
        pl.semaphore_signal(barrier, inc=1, device_id=(lat, lon), device_id_type=MESH)

    @pl.loop(1, Z)
    def _(d):
        pl.semaphore_signal(
            barrier, inc=1, device_id=(at(y, z_by(d), xh), j), device_id_type=MESH
        )

    def to_natural(src):
        for r in range(WIN_LAT):
            for c in range(WIN_LON):
                start = (r * WIN_LON + c) * LEVELS
                nat[start : start + LEVELS, :] = src[r, c]
        return nat[...]

    ready(fields, to_quarter)
    quads[...] = dot(to_quarter[...], to_natural(fields)).astype(BF16).reshape(4, QUAD, D)
    win[0] = quads[3]

    ready(split_shard, merge_shard)
    for k in range(KB):
        stack[8 * k : 8 * k + 8, :] = split_shard[:, MS * k : MS * (k + 1)].astype(F32)
    row = lax.broadcasted_iota(jnp.int32, (16, 64), 0)
    col = lax.broadcasted_iota(jnp.int32, (16, 64), 1)
    sel = (col == (row // 2) * 8 + 2 * j + row % 2).astype(F32).astype(BF16)
    raw[z] = dot(sel, stack[...].astype(BF16)).astype(BF16)
    own = lax.broadcasted_iota(jnp.int32, (1, MS), 1)
    place = ((own // (2 * Z * XH)) * Z + (own // 2) % Z) * XH + (own // (2 * Z)) % XH
    col = lax.broadcasted_iota(jnp.int32, (2 * D, MS), 0)
    sel = (col == 8 * place + 2 * j + own % 2).astype(F32).astype(BF16)
    merge_w[y, z, xh] = dot(merge_shard[...], sel).astype(BF16)

    pl.semaphore_wait(barrier, len(partners) + Z - 1)

    def roll_in(src, dst):
        return [
            push(src.at[(1 - a) * 2 + 1 - b], dst.at[a * 2 + b], lat_by(-a), lon_by(-b))
            for a, b in ((0, 1), (1, 0), (1, 1))
        ]

    def roll_out(src, dst):
        return [
            push(src.at[a * 2 + b], dst.at[(1 - a) * 2 + 1 - b], lat_by(a), lon_by(b))
            for a, b in ((0, 1), (1, 0), (1, 1))
        ]

    def z_copy(kind, d, src, dst):
        return pltpu.make_async_remote_copy(
            src_ref=src, dst_ref=dst, send_sem=zsend.at[kind, d], recv_sem=zrecv.at[kind, d],
            device_id=(at(y, z_by(d), xh), j), device_id_type=MESH,
        )

    def split_z(d):
        return z_copy(0, d, raw.at[z], raw.at[z])

    def merge_z(d):
        return z_copy(1, d, merge_w.at[y, z, xh], merge_w.at[y, z, xh])

    def sums_z(d):
        return z_copy(2, d, z_out.at[z_by(d)], z_in.at[z])

    def z_start(make):
        @pl.loop(1, Z)
        def _(d):
            make(d).start()

    def z_arrive(make):
        @pl.loop(1, Z)
        def _(d):
            make(d).wait_recv()

    fields_move = roll_in(quads, win)

    z_start(split_z)
    z_start(merge_z)

    def gather_start(whole):
        mine = whole.at[j]
        return push(mine, mine, i, across), push(mine, mine, i, mate)

    def gather_relay(whole, started):
        arrive(started[:1])
        came = whole.at[across]
        return started[1], push(came, came, i, mate)

    def reduce_start(src, mid):
        return push(src.at[mate], mid.at[0], i, mate), push(src.at[beyond], mid.at[1], i, mate)

    def reduce_cross(src, mid, started, slot):
        arrive(started)
        cross_out[slot] = (src[across].astype(F32) + mid[1].astype(F32)).astype(BF16)
        return [push(cross_out.at[slot], cross_in.at[slot], i, across)]

    def reduce_end(src, mid, crossed, slot):
        arrive(crossed)
        return src[j].astype(F32) + mid[0].astype(F32) + cross_in[slot].astype(F32)

    def lanes(rows):
        return jnp.concatenate([rows[QUAD * s : QUAD * (s + 1)] for s in range(4)], axis=1)

    def stacked(wide):
        return jnp.concatenate([wide[:, D * s : D * (s + 1)] for s in range(4)], axis=0)

    ready(cotangent, to_pair)
    cot_all[j] = lanes(dot(to_pair[...], to_natural(cotangent)).astype(BF16))

    arrive(fields_move)
    rolled = win[...].reshape(ROWS, D).astype(F32)
    ready(gain, inner)
    unit, scale = norm_parts(rolled)
    unit_keep[...] = unit
    normed[...] = (unit * gain[...]).astype(BF16)
    proj[...] = dot(normed[...], inner[...]).astype(BF16)

    ready(table, pick)
    make_bias(table, padded, pick[...], bias)

    full = Z * 16
    out = lax.broadcasted_iota(jnp.int32, (full, 1), 0)
    src = lax.broadcasted_iota(jnp.int32, (full, full), 1)
    want = ((out % (2 * Z)) // 2) * 16 + (out // (2 * Z)) * 2 + out % 2
    regroup = (src == want).astype(F32).astype(BF16)
    z_arrive(split_z)
    split_w[y, xh] = dot(regroup, raw[...].reshape(full, MS)).astype(BF16).reshape(KB, 2 * Z, MS)
    split_x = push(split_w.at[y, xh], split_w.at[y, xh], at(y, z, other), j)
    z_arrive(merge_z)
    merge_x = push(merge_w.at[y, :, xh], merge_w.at[y, :, xh], at(y, z, other), j)

    def y_spread(whole):
        return [push(whole.at[y], whole.at[y], at(y_by(d), z, xh), j) for d in (1, -1)]

    arrive([split_x])
    split_y = y_spread(split_w)
    cot_move = gather_start(cot_all)

    half_q = lax.broadcasted_iota(jnp.int32, (ROWS, 1), 0) // (2 * QUAD)
    half_k = lax.broadcasted_iota(jnp.int32, (1, ROWS), 1) // (2 * QUAD)
    allowed = jnp.logical_or(half_q == half_k, i != lat_size - 1)
    first = lax.broadcasted_iota(jnp.int32, (ROWS, HD2), 1) < HD2 // 2
    inv_root = (HD2 // 2) ** -0.5

    def of_head(values, h):
        return jnp.where(first if h % 2 == 0 else jnp.logical_not(first), values, jnp.zeros_like(values))

    def attend(pair):
        at_q = slice(HD2 * pair, HD2 * (pair + 1))
        at_k = slice(D + HD2 * pair, D + HD2 * (pair + 1))
        at_v = slice(2 * D + HD2 * pair, 2 * D + HD2 * (pair + 1))
        q, k, v = proj[:, at_q], proj[:, at_k], proj[:, at_v]
        results = []
        for h in (2 * pair, 2 * pair + 1):
            scores = dot(of_head(q, h), k, NT) * inv_root + bias[h]
            scores = jnp.where(allowed, scores, FAR)
            weights = jnp.exp(scores - jnp.max(scores, axis=-1, keepdims=True))
            weights = weights / jnp.sum(weights, axis=-1, keepdims=True)
            att[h] = weights
            results.append(dot(weights.astype(BF16), v))
        return jnp.where(first, results[0], results[1]).astype(BF16)

    attended = [attend(0), attend(1)]

    arrive([merge_x])
    merge_y = y_spread(merge_w)

    row = lax.broadcasted_iota(jnp.int32, (D, D), 0)
    col = lax.broadcasted_iota(jnp.int32, (1, D), 1)
    block = col // (4 * Z)
    want = ((block // XH) * Z + (col // 4) % Z) * (4 * XH) + (block % XH) * 4 + col % 4
    swap = (row == want).astype(F32).astype(BF16)
    ready(dense)
    toks = dot(dense[...], normed[...]).astype(BF16)
    toks_all[j] = dot(toks, swap).astype(BF16)
    toks_move = gather_start(toks_all)

    attended += [attend(2), attend(3)]
    attended = jnp.concatenate(attended, axis=1)
    ready(outer)
    y_rolled = (rolled + dot(attended, outer[...])).astype(BF16)
    y_out[...] = y_rolled.reshape(4, QUAD, D)
    y_in[3] = y_out[0]
    y_move = roll_out(y_out, y_in)

    def y_forward(whole, halves):
        return [
            push(halves(whole, y_by(-1), 0), halves(whole, y_by(-1), 0), at(y_by(1), z, xh), j),
            push(halves(whole, y_by(1), 1), halves(whole, y_by(1), 1), at(y_by(-1), z, xh), j),
        ]

    arrive(split_y)
    split_f = y_forward(split_w, lambda w, yy, part: w.at[yy, part])
    cot_rest = gather_relay(cot_all, cot_move)

    arrive(y_move)
    ready(pair_of_quarter, merge_gain)
    y_pairs = lanes(dot(pair_of_quarter[...], y_in[...].reshape(ROWS, D)))
    pair_unit, pair_scale = norm_parts(y_pairs)
    norm_all[j] = (pair_unit * merge_gain[...]).astype(BF16)
    norm_move = gather_start(norm_all)

    arrive(merge_y)
    merge_f = y_forward(merge_w, lambda w, yy, part: w.at[yy, pl.ds(part * (Z // 2), Z // 2)])

    arrive(cot_rest)
    arrive(split_f)

    def split_block(k):
        return split_w[:, :, k].reshape(MS, MS)

    cots = cot_all[...].reshape(lon_size * QUAD, 4 * D)
    grad_merged = dot(cots[:, :MS], split_block(0), NT)
    for k in range(1, KB):
        grad_merged = grad_merged + dot(cots[:, MS * k : MS * (k + 1)], split_block(k), NT)
    grad_merged = grad_merged.astype(BF16)
    arrive(merge_f)
    merge_full = merge_w[...].reshape(4 * D, MS)
    gm_out[...] = dot(grad_merged, merge_full, NT).astype(BF16).reshape(lon_size, QUAD, 4 * D)

    gm_start = reduce_start(gm_out, gm_mid)
    gm_crossed = reduce_cross(gm_out, gm_mid, gm_start, 0)
    norm_rest = gather_relay(norm_all, norm_move)
    toks_rest = gather_relay(toks_all, toks_move)

    grad_mnorm = reduce_end(gm_out, gm_mid, gm_crossed, 0)
    grad_y = cot_all[j].astype(F32) + norm_back(pair_unit, pair_scale, grad_mnorm, merge_gain[...])
    grad_y = dot(pair_of_quarter[...], stacked(grad_y.astype(BF16)), TN).astype(BF16)
    gy_out[...] = grad_y.reshape(4, QUAD, D)
    gy_in[0] = gy_out[3]
    gy_move = roll_in(gy_out, gy_in)

    arrive(norm_rest)
    merged = dot(norm_all[...].reshape(lon_size * QUAD, 4 * D), merge_full).astype(BF16)
    for k in range(KB):
        part = dot(merged, split_block(k)).astype(BF16)
        so_out[:, :, MS * k : MS * (k + 1)] = part.reshape(lon_size, QUAD, MS)
    so_start = reduce_start(so_out, so_mid)

    arrive(gy_move)
    grad_rolled_y = gy_in[...].reshape(ROWS, D)
    grad_attended = dot(grad_rolled_y, outer[...], NT).astype(BF16)
    for pair in range(HEADS // 2):
        at_q = slice(HD2 * pair, HD2 * (pair + 1))
        at_k = slice(D + HD2 * pair, D + HD2 * (pair + 1))
        at_v = slice(2 * D + HD2 * pair, 2 * D + HD2 * (pair + 1))
        q, k, v = proj[:, at_q], proj[:, at_k], proj[:, at_v]
        g = grad_attended[:, at_q]
        found = []
        for h in (2 * pair, 2 * pair + 1):
            weights = att[h]
            grad_p = dot(of_head(g, h), v, NT)
            grad_v = dot(weights.astype(BF16), g, TN)
            shared = jnp.sum(weights * grad_p, axis=-1, keepdims=True)
            grad_s = (weights * (grad_p - shared)).astype(BF16)
            found.append((dot(grad_s, k) * inv_root, dot(grad_s, q, TN) * inv_root, grad_v))
        for where, even, odd in zip((at_q, at_k, at_v), *found):
            gp[:, where] = jnp.where(first, even, odd).astype(BF16)
    few = dot(dense[...], gp[...]).astype(BF16)
    for d in range(lon_size):
        gp_out[d] = few[:, CW * d : CW * (d + 1)]
    gp_far = push(gp_out.at[beyond], gp_mid, i, across)
    gp_move = [
        push(gp_out.at[across], gp_in.at[j], i, across),
        push(gp_out.at[mate], gp_in.at[j], i, mate),
    ]
    gp_in[j] = gp_out[j]

    grad_normed = dot(gp[...], inner[...], NT)
    grad_in = grad_rolled_y.astype(F32) + norm_back(unit_keep[...], scale, grad_normed, gain[...])
    gf_out[...] = grad_in.astype(BF16).reshape(4, QUAD, D)
    gf_in[3] = gf_out[0]
    gf_move = roll_out(gf_out, gf_in)

    arrive([gp_far])
    gp_move.append(push(gp_mid, gp_in.at[across], i, mate))
    so_crossed = reduce_cross(so_out, so_mid, so_start, 1)

    arrive(toks_rest)
    arrive(gp_move)
    tokens = lon_size * WIN
    summed = dot(toks_all[...].reshape(tokens, D), gp_in[...].reshape(tokens, CW), TN)
    dw_out[...] = summed.astype(BF16).reshape(Y * XH, 4 * Z, CW)
    dw_move = []
    for dy, dx in plane:
        yy, xx = y_by(dy), lax.rem(xh + dx, XH)
        dw_move.append(push(dw_out.at[yy * XH + xx], dw_in.at[y * XH + xh], at(yy, z, xx), j))

    def from_pairs(wide):
        return dot(to_pair[...], stacked(wide), TN).astype(BF16)

    def put(dst, rows):
        for r in range(WIN_LAT):
            for c in range(WIN_LON):
                start = (r * WIN_LON + c) * LEVELS
                dst[r, c] = rows[start : start + LEVELS]

    split_out = reduce_end(so_out, so_mid, so_crossed, 1)
    put(outputs, from_pairs((y_pairs + split_out).astype(BF16)))

    arrive(dw_move)
    mine = dw_out[y * XH + xh].astype(F32)
    for dy, dx in plane:
        slot = y_by(-dy) * XH + lax.rem(xh + dx, XH)
        mine = mine + dw_in[slot].astype(F32)
    mine = mine.astype(BF16)
    CB = CW // 3
    tall = jnp.concatenate([mine[:, CB * c : CB * (c + 1)] for c in range(3)], axis=0)
    row = lax.broadcasted_iota(jnp.int32, (16 * Z, 1), 0)
    col = lax.broadcasted_iota(jnp.int32, (16 * Z, 12 * Z), 1)
    inner_row = row % 16
    want = (inner_row // 4) * (4 * Z) + (row // 16) * 4 + inner_row % 4
    spread = jnp.logical_and(col == want, inner_row < 12).astype(F32).astype(BF16)
    z_out[...] = dot(spread, tall).astype(BF16).reshape(Z, 16, CB)
    z_start(sums_z)
    z_in[z] = z_out[z]

    arrive(gf_move)
    put(grad_fields, dot(to_quarter[...], gf_in[...].reshape(ROWS, D), TN).astype(BF16))

    z_arrive(sums_z)
    owned = jnp.sum(z_in[...].astype(F32), axis=0)
    shrink = 1.0 / math.sqrt(WIN * lat_size * lon_size)
    for c in range(3):
        grad_inner[:, CB * c : CB * (c + 1)] = owned[4 * c : 4 * c + 4] * shrink

    for copy in sent:
        copy.wait_send()

    @pl.loop(1, Z)
    def _(d):
        split_z(d).wait_send()
        merge_z(d).wait_send()
        sums_z(d).wait_send()


def local(
    lon_size, fields, cotangent, norm_gain, inner_weight, outer_weight, bias_table, merge_gain,
    merge_weight, split_weight,
):
    D = fields.shape[-1]
    to_quarter, to_pair, pair_of_quarter, dense, pick = (jnp.asarray(a) for a in orders())
    vmem = pl.BlockSpec(memory_space=pltpu.VMEM)
    operands = (
        fields.transpose(1, 2, 0, 3), to_quarter, split_weight, merge_weight,
        cotangent.transpose(1, 2, 0, 3), to_pair, norm_gain.reshape(1, D), inner_weight, bias_table,
        pick, outer_weight, pair_of_quarter, merge_gain.reshape(1, 4 * D), dense,
    )
    MS, CW = D // 2, 3 * D // lon_size

    def buf(*shape, dtype=BF16):
        return pltpu.VMEM(shape, dtype)

    quarters = (4, QUAD, D)
    wide = (lon_size, QUAD, 4 * D)
    scratch = [
        buf(WIN, D), buf(*quarters), buf(*quarters), buf(*wide), buf(*wide),
        buf(Z, 16, MS), buf(64, MS, dtype=F32), buf(Y, XH, 8, 2 * Z, MS),
        buf(Y, Z, XH, 16, MS),
        buf(*quarters), buf(*quarters), buf(*wide), buf(*quarters), buf(*quarters),
        buf(*quarters), buf(*quarters), buf(HEADS, ROWS, ROWS, dtype=F32), buf(ROWS, 3 * D),
        buf(ROWS, D),
        buf(lon_size, WIN, D), buf(ROWS, 3 * D), buf(lon_size, WIN, CW), buf(lon_size, WIN, CW),
        buf(Y * XH, 4 * Z, CW), buf(Y * XH, 4 * Z, CW), buf(Z, 16, CW // 3), buf(Z, 16, CW // 3),
        buf(*wide), buf(ROWS, D, dtype=F32), buf(HEADS, ROWS, ROWS, dtype=F32),
        buf(HEADS, 2 * SPAN, dtype=F32), buf(WIN, CW),
        buf(2, QUAD, 4 * D), buf(2, QUAD, 4 * D), buf(2, QUAD, 4 * D), buf(2, QUAD, 4 * D),
    ]
    count = 64
    scratch += [
        pltpu.SemaphoreType.DMA((count,)), pltpu.SemaphoreType.DMA((count,)),
        pltpu.SemaphoreType.DMA((3, Z)), pltpu.SemaphoreType.DMA((3, Z)),
        pltpu.SemaphoreType.DMA((len(operands),)),
    ]
    scratch += [pltpu.VMEM(x.shape, x.dtype) for x in operands]
    grid_shape = (WIN_LAT, WIN_LON, LEVELS, D)
    out, grad, sums = pl.pallas_call(
        functools.partial(main_kernel, lon_size),
        out_shape=(
            jax.ShapeDtypeStruct(grid_shape, BF16),
            jax.ShapeDtypeStruct(grid_shape, BF16),
            jax.ShapeDtypeStruct((4, CW), F32),
        ),
        in_specs=[pl.BlockSpec(memory_space=pltpu.HBM)] * len(operands),
        out_specs=(vmem,) * 3,
        scratch_shapes=scratch,
        compiler_params=pltpu.CompilerParams(
            collective_id=0, has_side_effects=True, vmem_limit_bytes=63 * 1024 * 1024
        ),
    )(
        *operands,
    )
    return out.transpose(2, 0, 1, 3), grad.transpose(2, 0, 1, 3), sums


def solution(mesh):
    return jax.shard_map(
        functools.partial(local, mesh.shape["lon"]),
        mesh=mesh,
        in_specs=(
            P(None, "lat", "lon", None),
            P(None, "lat", "lon", None),
            P(),
            P(),
            P(),
            P(),
            P(),
            P("lat", None),
            P("lat", None),
        ),
        out_specs=(P(None, "lat", "lon", None), P(None, "lat", "lon", None), P("lat", "lon")),
        check_vma=False,
    )
```

```python
import functools
import math

import jax
import jax.numpy as jnp
import ml_dtypes
import numpy as np
from jax import lax
from jax.experimental import pallas as pl
from jax.experimental.pallas import tpu as pltpu
from jax.sharding import PartitionSpec as P

LEVELS = 2
WIN_LAT = 6
WIN_LON = 12
HEADS = 8
RELS = 759
SPAN = 384
QUAD = 48
ROWS = 4 * QUAD
WIN = 144
FAR = -1e30
Y, Z, XH = 4, 16, 2
FIRST = (6, -6, 3, -3, 8, 1, -1)
Z_FAR_FIRST = sorted(range(1, Z), key=lambda d: -min(d, Z - d))
SECOND = ((-1, 1), (1, -1), (-3, 1), (3, -1), (6, 1), (-6, -1), (-6, 1), (6, -1))
MESH = pl.DeviceIdType.MESH
NT = (((1,), (1,)), ((), ()))
TN = (((0,), (0,)), ((), ()))
F32 = jnp.float32
BF16 = jnp.bfloat16


def dot(a, b, dims=(((1,), (0,)), ((), ()))):
    return lax.dot_general(a, b, dims, preferred_element_type=F32)


def orders():
    natural, quarter, pair = {}, {}, {}
    base, compact = {}, {}
    for l in range(LEVELS):
        for r in range(WIN_LAT):
            for c in range(WIN_LON):
                token = (l, r, c)
                natural[token] = (r * WIN_LON + c) * LEVELS + l
                inside = (l * 3 + r % 3) * 6 + c % 6
                quarter[token] = ((r // 3) * 2 + c // 6) * QUAD + inside
                compact[token] = ((r // 3) * 2 + c // 6) * 36 + inside
                pair[token] = ((r % 2) * 2 + c % 2) * QUAD + (l * 3 + r // 2) * 6 + c // 2
                base[token] = (l * (2 * WIN_LAT - 1) + r) * (2 * WIN_LON - 1) + c
    to_quarter = np.zeros((ROWS, WIN), ml_dtypes.bfloat16)
    to_pair = np.zeros((ROWS, WIN), ml_dtypes.bfloat16)
    pair_of_quarter = np.zeros((ROWS, ROWS), ml_dtypes.bfloat16)
    dense = np.zeros((WIN, ROWS), ml_dtypes.bfloat16)
    pick = np.zeros((ROWS, SPAN), ml_dtypes.bfloat16)
    for token in natural:
        to_quarter[quarter[token], natural[token]] = 1
        to_pair[pair[token], natural[token]] = 1
        pair_of_quarter[pair[token], quarter[token]] = 1
        dense[compact[token], quarter[token]] = 1
        pick[quarter[token], base[token]] = 1
    return to_quarter, to_pair, pair_of_quarter, dense, pick


def make_bias(table_ref, padded_ref, pick, bias_ref):
    middle = (RELS - 1) // 2
    padded_ref[...] = jnp.zeros((HEADS, 2 * SPAN), F32)
    padded_ref[:, :RELS] = table_ref[...]
    back = 2 * SPAN - middle
    padded_ref[...] = pltpu.roll(padded_ref[...], back % 128, 1)
    used = jnp.sum(dot(jnp.ones((8, SPAN), BF16), pick, NT), axis=0, keepdims=True) > 0.5
    for h in range(HEADS):
        row = jnp.broadcast_to(padded_ref[h : h + 1, :], (SPAN, 2 * SPAN))
        shifted = pltpu.roll(row, back // 128 * 128, 1, stride=1, stride_axis=0)[:, :SPAN]
        high = shifted.astype(BF16)
        rest = shifted - high.astype(F32)
        middle_part = rest.astype(BF16)
        low = (rest - middle_part.astype(F32)).astype(BF16)
        total = jnp.zeros((ROWS, ROWS), F32)
        for part in (low, middle_part, high):
            total = total + dot(dot(pick, part, NT).astype(BF16), pick, NT)
        bias_ref[h] = jnp.where(used, total, FAR)


def norm_parts(values):
    mean = jnp.mean(values, axis=-1, keepdims=True)
    centred = values - mean
    variance = jnp.mean(centred * centred, axis=-1, keepdims=True)
    scale = lax.rsqrt(variance + 1e-05)
    return centred * scale, scale


def norm_back(unit, scale, grad, gain):
    g = grad * gain
    middle = jnp.mean(g, axis=-1, keepdims=True)
    along = jnp.mean(g * unit, axis=-1, keepdims=True)
    return scale * (g - middle - unit * along)


def main_kernel(
    lon_size,
    *refs,
):
    operands, refs = refs[:14], refs[14:]
    (
        outputs, grad_fields, grad_inner,
        nat, quads, win, cot_all, norm_all, raw, stack, split_w, merge_w,
        y_out, y_in, gm_out, gy_out, gy_in, gf_out, gf_in, att, proj, normed,
        toks_all, gp, gp_out, gp_in, dw_out, dw_in, z_out, z_in, so_out, unit_keep,
        bias, padded, gp_mid, gm_mid, so_mid, cross_out, cross_in,
        ssem, rsem, zsend, zrecv, lsem,
        *local_refs,
    ) = refs
    loads = [
        pltpu.make_async_copy(src, dst, lsem.at[k])
        for k, (src, dst) in enumerate(zip(operands, local_refs))
    ]
    for load in loads:
        load.start()
    (
        split_shard, merge_shard, fields, to_quarter, cotangent, to_pair, gain, inner, table,
        pick, outer, pair_of_quarter, merge_gain, dense,
    ) = local_refs
    loads = dict(zip(map(id, local_refs), loads))

    def ready(*wanted):
        for ref in wanted:
            loads[id(ref)].wait()

    D = fields.shape[-1]
    MS = D // 2
    CW = 3 * D // lon_size
    KB = 8
    HD2 = 2 * D // HEADS
    i, j = lax.axis_index("lat"), lax.axis_index("lon")
    lat_size = Y * Z * XH
    xh = lax.rem(i, XH)
    z = lax.rem(i // XH, Z)
    y = i // (XH * Z)
    other = lax.rem(xh + 1, XH)
    mate = j + 1 - 2 * lax.rem(j, 2)
    across = lax.rem(j + 2, lon_size)
    beyond = lax.rem(mate + 2, lon_size)

    def at(yy, zz, xx):
        return (yy * Z + zz) * XH + xx

    def lat_by(d):
        return lax.rem(i + d + lat_size, lat_size)

    def lon_by(d):
        return lax.rem(j + d + lon_size, lon_size)

    def y_by(d):
        return lax.rem(y + d + Y, Y)

    def z_by(d):
        return lax.rem(z + d, Z)

    sems = iter(range(ssem.shape[0]))
    sent = []

    def push(src, dst, lat, lon):
        k = next(sems)
        copy = pltpu.make_async_remote_copy(
            src_ref=src, dst_ref=dst, send_sem=ssem.at[k], recv_sem=rsem.at[k],
            device_id=(lat, lon), device_id_type=MESH,
        )
        copy.start()
        sent.append(copy)
        return copy

    def arrive(copies):
        for copy in copies:
            copy.wait_recv()

    partners = []
    for a, b in ((0, 1), (1, 0), (1, 1)):
        partners += [(lat_by(a), lon_by(b)), (lat_by(-a), lon_by(-b))]
    for d in range(1, lon_size):
        partners.append((i, lon_by(d)))
    plane = [(dy, dx) for dy in range(Y) for dx in range(XH) if dy or dx]
    for dy, dx in plane:
        partners.append((at(y_by(dy), z, lax.rem(xh + dx, XH)), j))
    barrier = pltpu.get_barrier_semaphore()
    partners = [(at(y, z_by(d), xh), j) for d in Z_FAR_FIRST] + partners
    for lat, lon in partners:
        pl.semaphore_signal(barrier, inc=1, device_id=(lat, lon), device_id_type=MESH)

    ready(split_shard, merge_shard)
    for k in range(KB):
        stack[8 * k : 8 * k + 8, :] = split_shard[:, MS * k : MS * (k + 1)].astype(F32)
    row = lax.broadcasted_iota(jnp.int32, (16, 64), 0)
    col = lax.broadcasted_iota(jnp.int32, (16, 64), 1)
    sel = (col == (row // 2) * 8 + 2 * j + row % 2).astype(F32).astype(BF16)
    raw[z] = dot(sel, stack[...].astype(BF16)).astype(BF16)
    own = lax.broadcasted_iota(jnp.int32, (1, MS), 1)
    place = ((own // (2 * Z * XH)) * Z + (own // 2) % Z) * XH + (own // (2 * Z)) % XH
    col = lax.broadcasted_iota(jnp.int32, (2 * D, MS), 0)
    sel = (col == 8 * place + 2 * j + own % 2).astype(F32).astype(BF16)
    merge_w[y, z, xh] = dot(merge_shard[...], sel).astype(BF16)

    pl.semaphore_wait(barrier, len(partners))

    def roll_in(src, dst):
        return [
            push(src.at[(1 - a) * 2 + 1 - b], dst.at[a * 2 + b], lat_by(-a), lon_by(-b))
            for a, b in ((0, 1), (1, 0), (1, 1))
        ]

    def roll_out(src, dst):
        return [
            push(src.at[a * 2 + b], dst.at[(1 - a) * 2 + 1 - b], lat_by(a), lon_by(b))
            for a, b in ((0, 1), (1, 0), (1, 1))
        ]

    def z_send(kind, slot, r, d):
        block, k = slot(z_by(r)), (r - d) % Z
        pltpu.make_async_remote_copy(
            src_ref=block, dst_ref=block, send_sem=zsend.at[kind, k], recv_sem=zrecv.at[kind, k],
            device_id=(at(y, z_by(d % Z), xh), j), device_id_type=MESH,
        ).start()

    def z_wait(kind, slot, steps, received=True):
        for e in steps:
            block, k = slot(z_by(e % Z)), e % Z
            copy = pltpu.make_async_remote_copy(
                src_ref=block, dst_ref=block, send_sem=zsend.at[kind, k], recv_sem=zrecv.at[kind, k],
                device_id=(at(y, z_by(1), xh), j), device_id_type=MESH,
            )
            if received:
                copy.wait_recv()
            else:
                copy.wait_send()

    def raw_slot(k):
        return raw.at[k]

    def merge_slot(k):
        return merge_w.at[y, k, xh]

    def z_first(kind, slot):
        for d in FIRST:
            z_send(kind, slot, 0, d)

    def z_second(kind, slot):
        z_wait(kind, slot, [-d for d in FIRST if abs(d) < Z // 2])
        for r, d in SECOND:
            z_send(kind, slot, r % Z, d)

    def z_third(kind, slot):
        z_wait(kind, slot, [e for e in range(1, Z) if e not in [-d % Z for d in FIRST if abs(d) < Z // 2]])

    def sums_z(d):
        return pltpu.make_async_remote_copy(
            src_ref=z_out.at[z_by(d)], dst_ref=z_in.at[z], send_sem=zsend.at[2, d], recv_sem=zrecv.at[2, d],
            device_id=(at(y, z_by(d), xh), j), device_id_type=MESH,
        )

    z_first(0, raw_slot)
    z_first(1, merge_slot)

    def to_natural(src):
        for r in range(WIN_LAT):
            for c in range(WIN_LON):
                start = (r * WIN_LON + c) * LEVELS
                nat[start : start + LEVELS, :] = src[r, c]
        return nat[...]

    ready(fields, to_quarter)
    quads[...] = dot(to_quarter[...], to_natural(fields)).astype(BF16).reshape(4, QUAD, D)
    win[0] = quads[3]
    fields_move = roll_in(quads, win)

    def gather_start(whole):
        mine = whole.at[j]
        return push(mine, mine, i, across), push(mine, mine, i, mate)

    def gather_relay(whole, started):
        arrive(started[:1])
        came = whole.at[across]
        return started[1], push(came, came, i, mate)

    def reduce_start(src, mid):
        return push(src.at[mate], mid.at[0], i, mate), push(src.at[beyond], mid.at[1], i, mate)

    def reduce_cross(src, mid, started, slot):
        arrive(started)
        cross_out[slot] = (src[across].astype(F32) + mid[1].astype(F32)).astype(BF16)
        return [push(cross_out.at[slot], cross_in.at[slot], i, across)]

    def reduce_end(src, mid, crossed, slot):
        arrive(crossed)
        return src[j].astype(F32) + mid[0].astype(F32) + cross_in[slot].astype(F32)

    def lanes(rows):
        return jnp.concatenate([rows[QUAD * s : QUAD * (s + 1)] for s in range(4)], axis=1)

    def stacked(wide):
        return jnp.concatenate([wide[:, D * s : D * (s + 1)] for s in range(4)], axis=0)

    ready(cotangent, to_pair)
    cot_all[j] = lanes(dot(to_pair[...], to_natural(cotangent)).astype(BF16))

    ready(table, pick)
    make_bias(table, padded, pick[...], bias)
    z_second(0, raw_slot)
    z_second(1, merge_slot)
    arrive(fields_move)
    rolled = win[...].reshape(ROWS, D).astype(F32)
    ready(gain, inner)
    unit, scale = norm_parts(rolled)
    unit_keep[...] = unit
    normed[...] = (unit * gain[...]).astype(BF16)
    proj[...] = dot(normed[...], inner[...]).astype(BF16)

    full = Z * 16
    out = lax.broadcasted_iota(jnp.int32, (full, 1), 0)
    src = lax.broadcasted_iota(jnp.int32, (full, full), 1)
    want = ((out % (2 * Z)) // 2) * 16 + (out // (2 * Z)) * 2 + out % 2
    regroup = (src == want).astype(F32).astype(BF16)
    z_third(0, raw_slot)
    split_w[y, xh] = dot(regroup, raw[...].reshape(full, MS)).astype(BF16).reshape(KB, 2 * Z, MS)
    split_x = push(split_w.at[y, xh], split_w.at[y, xh], at(y, z, other), j)
    z_third(1, merge_slot)
    merge_x = push(merge_w.at[y, :, xh], merge_w.at[y, :, xh], at(y, z, other), j)

    def y_spread(whole):
        return [push(whole.at[y], whole.at[y], at(y_by(d), z, xh), j) for d in (1, -1)]

    arrive([split_x])
    split_y = y_spread(split_w)

    half_q = lax.broadcasted_iota(jnp.int32, (ROWS, 1), 0) // (2 * QUAD)
    half_k = lax.broadcasted_iota(jnp.int32, (1, ROWS), 1) // (2 * QUAD)
    allowed = jnp.logical_or(half_q == half_k, i != lat_size - 1)
    first = lax.broadcasted_iota(jnp.int32, (ROWS, HD2), 1) < HD2 // 2
    inv_root = (HD2 // 2) ** -0.5

    def of_head(values, h):
        return jnp.where(first if h % 2 == 0 else jnp.logical_not(first), values, jnp.zeros_like(values))

    def attend(pair):
        at_q = slice(HD2 * pair, HD2 * (pair + 1))
        at_k = slice(D + HD2 * pair, D + HD2 * (pair + 1))
        at_v = slice(2 * D + HD2 * pair, 2 * D + HD2 * (pair + 1))
        q, k, v = proj[:, at_q], proj[:, at_k], proj[:, at_v]
        results = []
        for h in (2 * pair, 2 * pair + 1):
            scores = dot(of_head(q, h), k, NT) * inv_root + bias[h]
            scores = jnp.where(allowed, scores, FAR)
            weights = jnp.exp(scores - jnp.max(scores, axis=-1, keepdims=True))
            weights = weights / jnp.sum(weights, axis=-1, keepdims=True)
            att[h] = weights
            results.append(dot(weights.astype(BF16), v))
        return jnp.where(first, results[0], results[1]).astype(BF16)

    attended = [attend(0), attend(1)]

    arrive([merge_x])
    merge_y = y_spread(merge_w)
    cot_move = gather_start(cot_all)

    attended += [attend(2), attend(3)]
    attended = jnp.concatenate(attended, axis=1)
    ready(outer)
    y_rolled = (rolled + dot(attended, outer[...])).astype(BF16)
    y_out[...] = y_rolled.reshape(4, QUAD, D)
    y_in[3] = y_out[0]
    y_move = roll_out(y_out, y_in)

    row = lax.broadcasted_iota(jnp.int32, (D, D), 0)
    col = lax.broadcasted_iota(jnp.int32, (1, D), 1)
    block = col // (4 * Z)
    want = ((block // XH) * Z + (col // 4) % Z) * (4 * XH) + (block % XH) * 4 + col % 4
    swap = (row == want).astype(F32).astype(BF16)
    ready(dense)
    toks = dot(dense[...], normed[...]).astype(BF16)
    toks_all[j] = dot(toks, swap).astype(BF16)


    def y_forward(whole, halves):
        return [
            push(halves(whole, y_by(-1), 0), halves(whole, y_by(-1), 0), at(y_by(1), z, xh), j),
            push(halves(whole, y_by(1), 1), halves(whole, y_by(1), 1), at(y_by(-1), z, xh), j),
        ]

    arrive(split_y)
    split_f = y_forward(split_w, lambda w, yy, part: w.at[yy, part])
    cot_rest = gather_relay(cot_all, cot_move)

    arrive(y_move)
    ready(pair_of_quarter, merge_gain)
    y_pairs = lanes(dot(pair_of_quarter[...], y_in[...].reshape(ROWS, D)))
    pair_unit, pair_scale = norm_parts(y_pairs)
    norm_all[j] = (pair_unit * merge_gain[...]).astype(BF16)
    norm_move = gather_start(norm_all)
    toks_move = gather_start(toks_all)

    arrive(merge_y)
    merge_f = y_forward(merge_w, lambda w, yy, part: w.at[yy, pl.ds(part * (Z // 2), Z // 2)])

    arrive(cot_rest)
    arrive(split_f)

    def split_block(k):
        return split_w[:, :, k].reshape(MS, MS)

    cots = cot_all[...].reshape(lon_size * QUAD, 4 * D)
    grad_merged = dot(cots[:, :MS], split_block(0), NT)
    for k in range(1, KB):
        grad_merged = grad_merged + dot(cots[:, MS * k : MS * (k + 1)], split_block(k), NT)
    grad_merged = grad_merged.astype(BF16)
    arrive(merge_f)
    merge_full = merge_w[...].reshape(4 * D, MS)
    gm_out[...] = dot(grad_merged, merge_full, NT).astype(BF16).reshape(lon_size, QUAD, 4 * D)

    gm_start = reduce_start(gm_out, gm_mid)
    gm_crossed = reduce_cross(gm_out, gm_mid, gm_start, 0)
    norm_rest = gather_relay(norm_all, norm_move)
    toks_rest = gather_relay(toks_all, toks_move)

    grad_mnorm = reduce_end(gm_out, gm_mid, gm_crossed, 0)
    grad_y = cot_all[j].astype(F32) + norm_back(pair_unit, pair_scale, grad_mnorm, merge_gain[...])
    grad_y = dot(pair_of_quarter[...], stacked(grad_y.astype(BF16)), TN).astype(BF16)
    gy_out[...] = grad_y.reshape(4, QUAD, D)
    gy_in[0] = gy_out[3]
    gy_move = roll_in(gy_out, gy_in)

    arrive(norm_rest)
    merged = dot(norm_all[...].reshape(lon_size * QUAD, 4 * D), merge_full).astype(BF16)
    for k in range(KB):
        part = dot(merged, split_block(k)).astype(BF16)
        so_out[:, :, MS * k : MS * (k + 1)] = part.reshape(lon_size, QUAD, MS)
    so_start = reduce_start(so_out, so_mid)

    arrive(gy_move)
    so_crossed = reduce_cross(so_out, so_mid, so_start, 1)
    grad_rolled_y = gy_in[...].reshape(ROWS, D)
    grad_attended = dot(grad_rolled_y, outer[...], NT).astype(BF16)
    for pair in range(HEADS // 2):
        at_q = slice(HD2 * pair, HD2 * (pair + 1))
        at_k = slice(D + HD2 * pair, D + HD2 * (pair + 1))
        at_v = slice(2 * D + HD2 * pair, 2 * D + HD2 * (pair + 1))
        q, k, v = proj[:, at_q], proj[:, at_k], proj[:, at_v]
        g = grad_attended[:, at_q]
        found = []
        for h in (2 * pair, 2 * pair + 1):
            weights = att[h]
            grad_p = dot(of_head(g, h), v, NT)
            grad_v = dot(weights.astype(BF16), g, TN)
            shared = jnp.sum(weights * grad_p, axis=-1, keepdims=True)
            grad_s = (weights * (grad_p - shared)).astype(BF16)
            found.append((dot(grad_s, k) * inv_root, dot(grad_s, q, TN) * inv_root, grad_v))
        for where, even, odd in zip((at_q, at_k, at_v), *found):
            gp[:, where] = jnp.where(first, even, odd).astype(BF16)
    few = dot(dense[...], gp[...]).astype(BF16)
    for d in range(lon_size):
        gp_out[d] = few[:, CW * d : CW * (d + 1)]
    gp_far = push(gp_out.at[beyond], gp_mid, i, across)
    gp_move = [
        push(gp_out.at[across], gp_in.at[j], i, across),
        push(gp_out.at[mate], gp_in.at[j], i, mate),
    ]
    gp_in[j] = gp_out[j]

    grad_normed = dot(gp[...], inner[...], NT)
    grad_in = grad_rolled_y.astype(F32) + norm_back(unit_keep[...], scale, grad_normed, gain[...])
    gf_out[...] = grad_in.astype(BF16).reshape(4, QUAD, D)
    gf_in[3] = gf_out[0]
    gf_move = roll_out(gf_out, gf_in)

    arrive([gp_far])
    gp_move.append(push(gp_mid, gp_in.at[across], i, mate))

    arrive(toks_rest)
    arrive(gp_move[:2])
    summed = dot(toks_all[j], gp_in[j], TN) + dot(toks_all[mate], gp_in[mate], TN)
    summed = summed + dot(toks_all[across], gp_in[across], TN)
    arrive(gp_move[2:])
    summed = summed + dot(toks_all[beyond], gp_in[beyond], TN)
    dw_out[...] = summed.astype(BF16).reshape(Y * XH, 4 * Z, CW)
    dw_move = []
    for dy, dx in plane:
        yy, xx = y_by(dy), lax.rem(xh + dx, XH)
        dw_move.append(push(dw_out.at[yy * XH + xx], dw_in.at[y * XH + xh], at(yy, z, xx), j))

    def from_pairs(wide):
        return dot(to_pair[...], stacked(wide), TN).astype(BF16)

    def put(dst, rows):
        for r in range(WIN_LAT):
            for c in range(WIN_LON):
                start = (r * WIN_LON + c) * LEVELS
                dst[r, c] = rows[start : start + LEVELS]

    arrive(dw_move)
    mine = dw_out[y * XH + xh].astype(F32)
    for dy, dx in plane:
        slot = y_by(-dy) * XH + lax.rem(xh + dx, XH)
        mine = mine + dw_in[slot].astype(F32)
    mine = mine.astype(BF16)
    CB = CW // 3
    tall = jnp.concatenate([mine[:, CB * c : CB * (c + 1)] for c in range(3)], axis=0)
    row = lax.broadcasted_iota(jnp.int32, (16 * Z, 1), 0)
    col = lax.broadcasted_iota(jnp.int32, (16 * Z, 12 * Z), 1)
    inner_row = row % 16
    want = (inner_row // 4) * (4 * Z) + (row // 16) * 4 + inner_row % 4
    spread = jnp.logical_and(col == want, inner_row < 12).astype(F32).astype(BF16)
    z_out[...] = dot(spread, tall).astype(BF16).reshape(Z, 16, CB)

    for d in Z_FAR_FIRST:
        sums_z(d).start()
    z_in[z] = z_out[z]

    split_out = reduce_end(so_out, so_mid, so_crossed, 1)
    put(outputs, from_pairs((y_pairs + split_out).astype(BF16)))

    arrive(gf_move)
    put(grad_fields, dot(to_quarter[...], gf_in[...].reshape(ROWS, D), TN).astype(BF16))

    @pl.loop(1, Z)
    def _(d):
        sums_z(d).wait_recv()

    owned = jnp.sum(z_in[...].astype(F32), axis=0)
    shrink = 1.0 / math.sqrt(WIN * lat_size * lon_size)
    for c in range(3):
        grad_inner[:, CB * c : CB * (c + 1)] = owned[4 * c : 4 * c + 4] * shrink

    for copy in sent:
        copy.wait_send()

    @pl.loop(1, Z)
    def _(d):
        sums_z(d).wait_send()

    for kind, slot in enumerate((raw_slot, merge_slot)):
        z_wait(kind, slot, range(1, Z), received=False)


def settle_kernel(*refs):
    sources, targets, held, sems = refs[:3], refs[3:6], refs[6:9], refs[9]
    loads = [pltpu.make_async_copy(a, b, sems.at[0, k]) for k, (a, b) in enumerate(zip(sources, held))]
    stores = [pltpu.make_async_copy(a, b, sems.at[1, k]) for k, (a, b) in enumerate(zip(held, targets))]
    for load in loads:
        load.start()
    for load, store in zip(loads, stores):
        load.wait()
        store.start()
    for store in stores:
        store.wait()


def local(
    lon_size, fields, cotangent, norm_gain, inner_weight, outer_weight, bias_table, merge_gain,
    merge_weight, split_weight,
):
    D = fields.shape[-1]
    to_quarter, to_pair, pair_of_quarter, dense, pick = (jnp.asarray(a) for a in orders())
    vmem = pl.BlockSpec(memory_space=pltpu.VMEM)
    operands = (
        split_weight, merge_weight, fields.transpose(1, 2, 0, 3), to_quarter,
        cotangent.transpose(1, 2, 0, 3), to_pair, norm_gain.reshape(1, D), inner_weight, bias_table,
        pick, outer_weight, pair_of_quarter, merge_gain.reshape(1, 4 * D), dense,
    )
    MS, CW = D // 2, 3 * D // lon_size

    def buf(*shape, dtype=BF16):
        return pltpu.VMEM(shape, dtype)

    quarters = (4, QUAD, D)
    wide = (lon_size, QUAD, 4 * D)
    scratch = [
        buf(WIN, D), buf(*quarters), buf(*quarters), buf(*wide), buf(*wide),
        buf(Z, 16, MS), buf(64, MS, dtype=F32), buf(Y, XH, 8, 2 * Z, MS),
        buf(Y, Z, XH, 16, MS),
        buf(*quarters), buf(*quarters), buf(*wide), buf(*quarters), buf(*quarters),
        buf(*quarters), buf(*quarters), buf(HEADS, ROWS, ROWS, dtype=F32), buf(ROWS, 3 * D),
        buf(ROWS, D),
        buf(lon_size, WIN, D), buf(ROWS, 3 * D), buf(lon_size, WIN, CW), buf(lon_size, WIN, CW),
        buf(Y * XH, 4 * Z, CW), buf(Y * XH, 4 * Z, CW), buf(Z, 16, CW // 3), buf(Z, 16, CW // 3),
        buf(*wide), buf(ROWS, D, dtype=F32), buf(HEADS, ROWS, ROWS, dtype=F32),
        buf(HEADS, 2 * SPAN, dtype=F32), buf(WIN, CW),
        buf(2, QUAD, 4 * D), buf(2, QUAD, 4 * D), buf(2, QUAD, 4 * D), buf(2, QUAD, 4 * D),
    ]
    count = 64
    scratch += [
        pltpu.SemaphoreType.DMA((count,)), pltpu.SemaphoreType.DMA((count,)),
        pltpu.SemaphoreType.DMA((3, Z)), pltpu.SemaphoreType.DMA((3, Z)),
        pltpu.SemaphoreType.DMA((len(operands),)),
    ]
    scratch += [pltpu.VMEM(x.shape, x.dtype) for x in operands]
    grid_shape = (WIN_LAT, WIN_LON, LEVELS, D)
    out, grad, sums = pl.pallas_call(
        functools.partial(main_kernel, lon_size),
        out_shape=(
            jax.ShapeDtypeStruct(grid_shape, BF16),
            jax.ShapeDtypeStruct(grid_shape, BF16),
            jax.ShapeDtypeStruct((4, CW), F32),
        ),
        in_specs=[pl.BlockSpec(memory_space=pltpu.HBM)] * len(operands),
        out_specs=(vmem,) * 3,
        scratch_shapes=scratch,
        compiler_params=pltpu.CompilerParams(
            collective_id=0, has_side_effects=True, vmem_limit_bytes=63 * 1024 * 1024
        ),
    )(
        *operands,
    )
    results = (out, grad, sums)
    hbm = pl.BlockSpec(memory_space=pltpu.HBM)
    out, grad, sums = pl.pallas_call(
        settle_kernel,
        out_shape=tuple(jax.ShapeDtypeStruct(x.shape, x.dtype) for x in results),
        in_specs=[hbm] * 3,
        out_specs=(hbm,) * 3,
        scratch_shapes=[
            *(pltpu.VMEM(x.shape, x.dtype) for x in results),
            pltpu.SemaphoreType.DMA((2, 3)),
        ],
        compiler_params=pltpu.CompilerParams(vmem_limit_bytes=63 * 1024 * 1024),
    )(*results)
    return out.transpose(2, 0, 1, 3), grad.transpose(2, 0, 1, 3), sums


def solution(mesh):
    return jax.shard_map(
        functools.partial(local, mesh.shape["lon"]),
        mesh=mesh,
        in_specs=(
            P(None, "lat", "lon", None),
            P(None, "lat", "lon", None),
            P(),
            P(),
            P(),
            P(),
            P(),
            P("lat", None),
            P("lat", None),
        ),
        out_specs=(P(None, "lat", "lon", None), P(None, "lat", "lon", None), P("lat", "lon")),
        check_vma=False,
    )
```

```python
import functools
import math

import jax
import jax.numpy as jnp
import ml_dtypes
import numpy as np
from jax import lax
from jax.experimental import pallas as pl
from jax.experimental.pallas import tpu as pltpu
from jax.sharding import PartitionSpec as P

LEVELS = 2
WIN_LAT = 6
WIN_LON = 12
HEADS = 8
RELS = 759
SPAN = 384
QUAD = 48
ROWS = 4 * QUAD
WIN = 144
FAR = -1e30
Y, Z, XH = 4, 16, 2
FIRST = (6, -6, 3, -3, 8, 1, -1)
Z_FAR_FIRST = sorted(range(1, Z), key=lambda d: -min(d, Z - d))
SECOND = ((-1, 1), (1, -1), (-3, 1), (3, -1), (6, 1), (-6, -1), (-6, 1), (6, -1))
MESH = pl.DeviceIdType.MESH
NT = (((1,), (1,)), ((), ()))
TN = (((0,), (0,)), ((), ()))
F32 = jnp.float32
BF16 = jnp.bfloat16


def dot(a, b, dims=(((1,), (0,)), ((), ()))):
    return lax.dot_general(a, b, dims, preferred_element_type=F32)


def orders():
    natural, quarter, pair = {}, {}, {}
    base, compact = {}, {}
    for l in range(LEVELS):
        for r in range(WIN_LAT):
            for c in range(WIN_LON):
                token = (l, r, c)
                natural[token] = (r * WIN_LON + c) * LEVELS + l
                inside = (l * 3 + r % 3) * 6 + c % 6
                quarter[token] = ((r // 3) * 2 + c // 6) * QUAD + inside
                compact[token] = ((r // 3) * 2 + c // 6) * 36 + inside
                pair[token] = ((r % 2) * 2 + c % 2) * QUAD + (l * 3 + r // 2) * 6 + c // 2
                base[token] = (l * (2 * WIN_LAT - 1) + r) * (2 * WIN_LON - 1) + c
    to_quarter = np.zeros((ROWS, WIN), ml_dtypes.bfloat16)
    to_pair = np.zeros((ROWS, WIN), ml_dtypes.bfloat16)
    pair_of_quarter = np.zeros((ROWS, ROWS), ml_dtypes.bfloat16)
    dense = np.zeros((WIN, ROWS), ml_dtypes.bfloat16)
    pick = np.zeros((ROWS, SPAN), ml_dtypes.bfloat16)
    for token in natural:
        to_quarter[quarter[token], natural[token]] = 1
        to_pair[pair[token], natural[token]] = 1
        pair_of_quarter[pair[token], quarter[token]] = 1
        dense[compact[token], quarter[token]] = 1
        pick[quarter[token], base[token]] = 1
    return to_quarter, to_pair, pair_of_quarter, dense, pick


def make_bias(table_ref, padded_ref, pick, bias_ref):
    middle = (RELS - 1) // 2
    padded_ref[...] = jnp.zeros((HEADS, 2 * SPAN), F32)
    padded_ref[:, :RELS] = table_ref[...]
    back = 2 * SPAN - middle
    padded_ref[...] = pltpu.roll(padded_ref[...], back % 128, 1)
    used = jnp.sum(dot(jnp.ones((8, SPAN), BF16), pick, NT), axis=0, keepdims=True) > 0.5
    for h in range(HEADS):
        row = jnp.broadcast_to(padded_ref[h : h + 1, :], (SPAN, 2 * SPAN))
        shifted = pltpu.roll(row, back // 128 * 128, 1, stride=1, stride_axis=0)[:, :SPAN]
        high = shifted.astype(BF16)
        rest = shifted - high.astype(F32)
        middle_part = rest.astype(BF16)
        low = (rest - middle_part.astype(F32)).astype(BF16)
        total = jnp.zeros((ROWS, ROWS), F32)
        for part in (low, middle_part, high):
            total = total + dot(dot(pick, part, NT).astype(BF16), pick, NT)
        bias_ref[h] = jnp.where(used, total, FAR)


def norm_parts(values):
    mean = jnp.mean(values, axis=-1, keepdims=True)
    centred = values - mean
    variance = jnp.mean(centred * centred, axis=-1, keepdims=True)
    scale = lax.rsqrt(variance + 1e-05)
    return centred * scale, scale


def norm_back(unit, scale, grad, gain):
    g = grad * gain
    middle = jnp.mean(g, axis=-1, keepdims=True)
    along = jnp.mean(g * unit, axis=-1, keepdims=True)
    return scale * (g - middle - unit * along)


def main_kernel(
    lon_size,
    *refs,
):
    operands, refs = refs[:14], refs[14:]
    (
        outputs_hbm, grad_fields_hbm, grad_inner,
        nat, quads, win, cot_all, norm_all, raw, stack, split_w, merge_w,
        y_out, y_in, gm_out, gy_out, gy_in, gf_out, gf_in, att, proj, normed,
        toks_all, gp, gp_out, gp_in, dw_out, dw_in, z_out, z_in, so_out, unit_keep,
        bias, padded, gp_mid, gm_mid, so_mid, cross_out, cross_in,
        ssem, rsem, zsend, zrecv, lsem, outputs, grad_fields, osem,
        *local_refs,
    ) = refs
    loads = [
        pltpu.make_async_copy(src, dst, lsem.at[k])
        for k, (src, dst) in enumerate(zip(operands, local_refs))
    ]
    for load in loads:
        load.start()
    (
        split_shard, merge_shard, fields, to_quarter, cotangent, to_pair, gain, inner, table,
        pick, outer, pair_of_quarter, merge_gain, dense,
    ) = local_refs
    loads = dict(zip(map(id, local_refs), loads))

    def ready(*wanted):
        for ref in wanted:
            loads[id(ref)].wait()

    D = fields.shape[-1]
    MS = D // 2
    CW = 3 * D // lon_size
    KB = 8
    HD2 = 2 * D // HEADS
    i, j = lax.axis_index("lat"), lax.axis_index("lon")
    lat_size = Y * Z * XH
    xh = lax.rem(i, XH)
    z = lax.rem(i // XH, Z)
    y = i // (XH * Z)
    other = lax.rem(xh + 1, XH)
    mate = j + 1 - 2 * lax.rem(j, 2)
    across = lax.rem(j + 2, lon_size)
    beyond = lax.rem(mate + 2, lon_size)

    def at(yy, zz, xx):
        return (yy * Z + zz) * XH + xx

    def lat_by(d):
        return lax.rem(i + d + lat_size, lat_size)

    def lon_by(d):
        return lax.rem(j + d + lon_size, lon_size)

    def y_by(d):
        return lax.rem(y + d + Y, Y)

    def z_by(d):
        return lax.rem(z + d, Z)

    sems = iter(range(ssem.shape[0]))
    sent = []

    def push(src, dst, lat, lon):
        k = next(sems)
        copy = pltpu.make_async_remote_copy(
            src_ref=src, dst_ref=dst, send_sem=ssem.at[k], recv_sem=rsem.at[k],
            device_id=(lat, lon), device_id_type=MESH,
        )
        copy.start()
        sent.append(copy)
        return copy

    def arrive(copies):
        for copy in copies:
            copy.wait_recv()

    partners = []
    for a, b in ((0, 1), (1, 0), (1, 1)):
        partners += [(lat_by(a), lon_by(b)), (lat_by(-a), lon_by(-b))]
    for d in range(1, lon_size):
        partners.append((i, lon_by(d)))
    plane = [(dy, dx) for dy in range(Y) for dx in range(XH) if dy or dx]
    for dy, dx in plane:
        partners.append((at(y_by(dy), z, lax.rem(xh + dx, XH)), j))
    barrier = pltpu.get_barrier_semaphore()
    partners = [(at(y, z_by(d), xh), j) for d in Z_FAR_FIRST] + partners
    for lat, lon in partners:
        pl.semaphore_signal(barrier, inc=1, device_id=(lat, lon), device_id_type=MESH)

    ready(split_shard, merge_shard)
    for k in range(KB):
        stack[8 * k : 8 * k + 8, :] = split_shard[:, MS * k : MS * (k + 1)].astype(F32)
    row = lax.broadcasted_iota(jnp.int32, (16, 64), 0)
    col = lax.broadcasted_iota(jnp.int32, (16, 64), 1)
    sel = (col == (row // 2) * 8 + 2 * j + row % 2).astype(F32).astype(BF16)
    raw[z] = dot(sel, stack[...].astype(BF16)).astype(BF16)
    own = lax.broadcasted_iota(jnp.int32, (1, MS), 1)
    place = ((own // (2 * Z * XH)) * Z + (own // 2) % Z) * XH + (own // (2 * Z)) % XH
    col = lax.broadcasted_iota(jnp.int32, (2 * D, MS), 0)
    sel = (col == 8 * place + 2 * j + own % 2).astype(F32).astype(BF16)
    merge_w[y, z, xh] = dot(merge_shard[...], sel).astype(BF16)

    pl.semaphore_wait(barrier, len(partners))

    def roll_in(src, dst):
        return [
            push(src.at[(1 - a) * 2 + 1 - b], dst.at[a * 2 + b], lat_by(-a), lon_by(-b))
            for a, b in ((1, 1), (1, 0), (0, 1))
        ]

    def roll_out(src, dst):
        return [
            push(src.at[a * 2 + b], dst.at[(1 - a) * 2 + 1 - b], lat_by(a), lon_by(b))
            for a, b in ((1, 1), (1, 0), (0, 1))
        ]

    def z_send(kind, slot, r, d):
        block, k = slot(z_by(r)), (r - d) % Z
        pltpu.make_async_remote_copy(
            src_ref=block, dst_ref=block, send_sem=zsend.at[kind, k], recv_sem=zrecv.at[kind, k],
            device_id=(at(y, z_by(d % Z), xh), j), device_id_type=MESH,
        ).start()

    def z_wait(kind, slot, steps, received=True):
        for e in steps:
            block, k = slot(z_by(e % Z)), e % Z
            copy = pltpu.make_async_remote_copy(
                src_ref=block, dst_ref=block, send_sem=zsend.at[kind, k], recv_sem=zrecv.at[kind, k],
                device_id=(at(y, z_by(1), xh), j), device_id_type=MESH,
            )
            if received:
                copy.wait_recv()
            else:
                copy.wait_send()

    def raw_slot(k):
        return raw.at[k]

    def merge_slot(k):
        return merge_w.at[y, k, xh]

    def z_first(kind, slot):
        for d in FIRST:
            z_send(kind, slot, 0, d)

    def z_second(kind, slot):
        z_wait(kind, slot, [-d for d in FIRST if abs(d) < Z // 2])
        for r, d in SECOND:
            z_send(kind, slot, r % Z, d)

    def z_third(kind, slot):
        z_wait(kind, slot, [e for e in range(1, Z) if e not in [-d % Z for d in FIRST if abs(d) < Z // 2]])

    def sums_z(d):
        return pltpu.make_async_remote_copy(
            src_ref=z_out.at[z_by(d)], dst_ref=z_in.at[z], send_sem=zsend.at[2, d], recv_sem=zrecv.at[2, d],
            device_id=(at(y, z_by(d), xh), j), device_id_type=MESH,
        )

    z_first(0, raw_slot)
    z_first(1, merge_slot)

    def to_natural(src):
        for r in range(WIN_LAT):
            for c in range(WIN_LON):
                start = (r * WIN_LON + c) * LEVELS
                nat[start : start + LEVELS, :] = src[r, c]
        return nat[...]

    ready(fields, to_quarter)
    quads[...] = dot(to_quarter[...], to_natural(fields)).astype(BF16).reshape(4, QUAD, D)
    win[0] = quads[3]
    fields_move = roll_in(quads, win)

    def gather_start(whole):
        mine = whole.at[j]
        return push(mine, mine, i, across), push(mine, mine, i, mate)

    def gather_relay(whole, started):
        arrive(started[:1])
        came = whole.at[across]
        return started[1], push(came, came, i, mate)

    def reduce_start(src, mid):
        return push(src.at[beyond], mid.at[1], i, mate), push(src.at[mate], mid.at[0], i, mate)

    def reduce_cross(src, mid, started, slot):
        arrive(started[:1])
        cross_out[slot] = (src[across].astype(F32) + mid[1].astype(F32)).astype(BF16)
        return [started[1], push(cross_out.at[slot], cross_in.at[slot], i, across)]

    def reduce_end(src, mid, crossed, slot):
        arrive(crossed)
        return src[j].astype(F32) + mid[0].astype(F32) + cross_in[slot].astype(F32)

    def lanes(rows):
        return jnp.concatenate([rows[QUAD * s : QUAD * (s + 1)] for s in range(4)], axis=1)

    def stacked(wide):
        return jnp.concatenate([wide[:, D * s : D * (s + 1)] for s in range(4)], axis=0)

    ready(cotangent, to_pair)
    cot_all[j] = lanes(dot(to_pair[...], to_natural(cotangent)).astype(BF16))

    ready(table, pick)
    make_bias(table, padded, pick[...], bias)
    z_second(0, raw_slot)
    z_second(1, merge_slot)
    arrive(fields_move)
    rolled = win[...].reshape(ROWS, D).astype(F32)
    ready(gain, inner)
    unit, scale = norm_parts(rolled)
    unit_keep[...] = unit
    normed[...] = (unit * gain[...]).astype(BF16)
    proj[...] = dot(normed[...], inner[...]).astype(BF16)

    full = Z * 16
    out = lax.broadcasted_iota(jnp.int32, (full, 1), 0)
    src = lax.broadcasted_iota(jnp.int32, (full, full), 1)
    want = ((out % (2 * Z)) // 2) * 16 + (out // (2 * Z)) * 2 + out % 2
    regroup = (src == want).astype(F32).astype(BF16)
    z_third(0, raw_slot)
    split_w[y, xh] = dot(regroup, raw[...].reshape(full, MS)).astype(BF16).reshape(KB, 2 * Z, MS)
    split_x = push(split_w.at[y, xh], split_w.at[y, xh], at(y, z, other), j)
    z_third(1, merge_slot)
    merge_x = push(merge_w.at[y, :, xh], merge_w.at[y, :, xh], at(y, z, other), j)

    def y_spread(whole):
        return [push(whole.at[y], whole.at[y], at(y_by(d), z, xh), j) for d in (1, -1)]

    arrive([split_x])
    split_y = y_spread(split_w)

    half_q = lax.broadcasted_iota(jnp.int32, (ROWS, 1), 0) // (2 * QUAD)
    half_k = lax.broadcasted_iota(jnp.int32, (1, ROWS), 1) // (2 * QUAD)
    allowed = jnp.logical_or(half_q == half_k, i != lat_size - 1)
    first = lax.broadcasted_iota(jnp.int32, (ROWS, HD2), 1) < HD2 // 2
    inv_root = (HD2 // 2) ** -0.5

    def of_head(values, h):
        return jnp.where(first if h % 2 == 0 else jnp.logical_not(first), values, jnp.zeros_like(values))

    def attend(pair):
        at_q = slice(HD2 * pair, HD2 * (pair + 1))
        at_k = slice(D + HD2 * pair, D + HD2 * (pair + 1))
        at_v = slice(2 * D + HD2 * pair, 2 * D + HD2 * (pair + 1))
        q, k, v = proj[:, at_q], proj[:, at_k], proj[:, at_v]
        results = []
        for h in (2 * pair, 2 * pair + 1):
            scores = dot(of_head(q, h), k, NT) * inv_root + bias[h]
            scores = jnp.where(allowed, scores, FAR)
            weights = jnp.exp(scores - jnp.max(scores, axis=-1, keepdims=True))
            weights = weights / jnp.sum(weights, axis=-1, keepdims=True)
            att[h] = weights
            results.append(dot(weights.astype(BF16), v))
        return jnp.where(first, results[0], results[1]).astype(BF16)

    attended = [attend(0), attend(1)]

    arrive([merge_x])
    merge_y = y_spread(merge_w)
    cot_move = gather_start(cot_all)

    attended += [attend(2), attend(3)]
    attended = jnp.concatenate(attended, axis=1)
    ready(outer)
    y_rolled = (rolled + dot(attended, outer[...])).astype(BF16)
    y_out[...] = y_rolled.reshape(4, QUAD, D)
    y_in[3] = y_out[0]
    y_move = roll_out(y_out, y_in)

    row = lax.broadcasted_iota(jnp.int32, (D, D), 0)
    col = lax.broadcasted_iota(jnp.int32, (1, D), 1)
    block = col // (4 * Z)
    want = ((block // XH) * Z + (col // 4) % Z) * (4 * XH) + (block % XH) * 4 + col % 4
    swap = (row == want).astype(F32).astype(BF16)
    ready(dense)
    toks = dot(dense[...], normed[...]).astype(BF16)
    toks_all[j] = dot(toks, swap).astype(BF16)


    def y_forward(whole, halves):
        return [
            push(halves(whole, y_by(-1), 0), halves(whole, y_by(-1), 0), at(y_by(1), z, xh), j),
            push(halves(whole, y_by(1), 1), halves(whole, y_by(1), 1), at(y_by(-1), z, xh), j),
        ]

    arrive(split_y)
    split_f = y_forward(split_w, lambda w, yy, part: w.at[yy, part])
    cot_rest = gather_relay(cot_all, cot_move)

    arrive(y_move)
    ready(pair_of_quarter, merge_gain)
    y_pairs = lanes(dot(pair_of_quarter[...], y_in[...].reshape(ROWS, D)))
    pair_unit, pair_scale = norm_parts(y_pairs)
    norm_all[j] = (pair_unit * merge_gain[...]).astype(BF16)
    norm_move = gather_start(norm_all)
    toks_move = gather_start(toks_all)

    arrive(merge_y)
    merge_f = y_forward(merge_w, lambda w, yy, part: w.at[yy, pl.ds(part * (Z // 2), Z // 2)])

    arrive(cot_rest)
    arrive(split_f)

    def split_block(k):
        return split_w[:, :, k].reshape(MS, MS)

    cots = cot_all[...].reshape(lon_size * QUAD, 4 * D)
    grad_merged = dot(cots[:, :MS], split_block(0), NT)
    for k in range(1, KB):
        grad_merged = grad_merged + dot(cots[:, MS * k : MS * (k + 1)], split_block(k), NT)
    grad_merged = grad_merged.astype(BF16)
    arrive(merge_f)
    merge_full = merge_w[...].reshape(4 * D, MS)
    gm_out[...] = dot(grad_merged, merge_full, NT).astype(BF16).reshape(lon_size, QUAD, 4 * D)

    gm_start = reduce_start(gm_out, gm_mid)
    gm_crossed = reduce_cross(gm_out, gm_mid, gm_start, 0)
    norm_rest = gather_relay(norm_all, norm_move)
    toks_rest = gather_relay(toks_all, toks_move)

    grad_mnorm = reduce_end(gm_out, gm_mid, gm_crossed, 0)
    grad_y = cot_all[j].astype(F32) + norm_back(pair_unit, pair_scale, grad_mnorm, merge_gain[...])
    grad_y = dot(pair_of_quarter[...], stacked(grad_y.astype(BF16)), TN).astype(BF16)
    gy_out[...] = grad_y.reshape(4, QUAD, D)
    gy_in[0] = gy_out[3]
    gy_move = roll_in(gy_out, gy_in)

    arrive(norm_rest)
    merged = dot(norm_all[...].reshape(lon_size * QUAD, 4 * D), merge_full).astype(BF16)
    for k in range(KB):
        part = dot(merged, split_block(k)).astype(BF16)
        so_out[:, :, MS * k : MS * (k + 1)] = part.reshape(lon_size, QUAD, MS)
    so_start = reduce_start(so_out, so_mid)

    arrive(gy_move)
    so_crossed = reduce_cross(so_out, so_mid, so_start, 1)
    grad_rolled_y = gy_in[...].reshape(ROWS, D)
    grad_attended = dot(grad_rolled_y, outer[...], NT).astype(BF16)
    for pair in range(HEADS // 2):
        at_q = slice(HD2 * pair, HD2 * (pair + 1))
        at_k = slice(D + HD2 * pair, D + HD2 * (pair + 1))
        at_v = slice(2 * D + HD2 * pair, 2 * D + HD2 * (pair + 1))
        q, k, v = proj[:, at_q], proj[:, at_k], proj[:, at_v]
        g = grad_attended[:, at_q]
        found = []
        for h in (2 * pair, 2 * pair + 1):
            weights = att[h]
            grad_p = dot(of_head(g, h), v, NT)
            grad_v = dot(weights.astype(BF16), g, TN)
            shared = jnp.sum(weights * grad_p, axis=-1, keepdims=True)
            grad_s = (weights * (grad_p - shared)).astype(BF16)
            found.append((dot(grad_s, k) * inv_root, dot(grad_s, q, TN) * inv_root, grad_v))
        for where, even, odd in zip((at_q, at_k, at_v), *found):
            gp[:, where] = jnp.where(first, even, odd).astype(BF16)
    few = dot(dense[...], gp[...]).astype(BF16)
    for d in range(lon_size):
        gp_out[d] = few[:, CW * d : CW * (d + 1)]
    gp_far = push(gp_out.at[beyond], gp_mid, i, across)
    gp_move = [
        push(gp_out.at[across], gp_in.at[j], i, across),
        push(gp_out.at[mate], gp_in.at[j], i, mate),
    ]
    gp_in[j] = gp_out[j]

    grad_normed = dot(gp[...], inner[...], NT)
    grad_in = grad_rolled_y.astype(F32) + norm_back(unit_keep[...], scale, grad_normed, gain[...])
    gf_out[...] = grad_in.astype(BF16).reshape(4, QUAD, D)
    gf_in[3] = gf_out[0]
    gf_move = roll_out(gf_out, gf_in)

    arrive([gp_far])
    gp_move.append(push(gp_mid, gp_in.at[across], i, mate))

    arrive(toks_rest)
    arrive(gp_move[:2])
    summed = dot(toks_all[j], gp_in[j], TN) + dot(toks_all[mate], gp_in[mate], TN)
    summed = summed + dot(toks_all[across], gp_in[across], TN)
    arrive(gp_move[2:])
    summed = summed + dot(toks_all[beyond], gp_in[beyond], TN)
    dw_out[...] = summed.astype(BF16).reshape(Y * XH, 4 * Z, CW)
    dw_move = []
    for dy, dx in sorted(plane, key=lambda p: -min(p[0], Y - p[0]) - 2 * p[1]):
        yy, xx = y_by(dy), lax.rem(xh + dx, XH)
        dw_move.append(push(dw_out.at[yy * XH + xx], dw_in.at[y * XH + xh], at(yy, z, xx), j))

    def from_pairs(wide):
        return dot(to_pair[...], stacked(wide), TN).astype(BF16)

    def put(dst, rows):
        for r in range(WIN_LAT):
            for c in range(WIN_LON):
                start = (r * WIN_LON + c) * LEVELS
                dst[r, c] = rows[start : start + LEVELS]

    arrive(dw_move)
    mine = dw_out[y * XH + xh].astype(F32)
    for dy, dx in plane:
        slot = y_by(-dy) * XH + lax.rem(xh + dx, XH)
        mine = mine + dw_in[slot].astype(F32)
    mine = mine.astype(BF16)
    CB = CW // 3
    tall = jnp.concatenate([mine[:, CB * c : CB * (c + 1)] for c in range(3)], axis=0)
    row = lax.broadcasted_iota(jnp.int32, (16 * Z, 1), 0)
    col = lax.broadcasted_iota(jnp.int32, (16 * Z, 12 * Z), 1)
    inner_row = row % 16
    want = (inner_row // 4) * (4 * Z) + (row // 16) * 4 + inner_row % 4
    spread = jnp.logical_and(col == want, inner_row < 12).astype(F32).astype(BF16)
    z_out[...] = dot(spread, tall).astype(BF16).reshape(Z, 16, CB)

    for d in Z_FAR_FIRST:
        sums_z(d).start()
    z_in[z] = z_out[z]

    split_out = reduce_end(so_out, so_mid, so_crossed, 1)
    put(outputs, from_pairs((y_pairs + split_out).astype(BF16)))
    stores = [pltpu.make_async_copy(outputs, outputs_hbm, osem.at[0])]
    stores[0].start()

    arrive(gf_move)
    put(grad_fields, dot(to_quarter[...], gf_in[...].reshape(ROWS, D), TN).astype(BF16))
    stores.append(pltpu.make_async_copy(grad_fields, grad_fields_hbm, osem.at[1]))
    stores[1].start()

    @pl.loop(1, Z)
    def _(d):
        sums_z(d).wait_recv()

    owned = jnp.sum(z_in[...].astype(F32), axis=0)
    shrink = 1.0 / math.sqrt(WIN * lat_size * lon_size)
    for c in range(3):
        grad_inner[:, CB * c : CB * (c + 1)] = owned[4 * c : 4 * c + 4] * shrink

    for store in stores:
        store.wait()
    for copy in sent:
        copy.wait_send()

    @pl.loop(1, Z)
    def _(d):
        sums_z(d).wait_send()

    for kind, slot in enumerate((raw_slot, merge_slot)):
        z_wait(kind, slot, range(1, Z), received=False)


def settle_kernel(*refs):
    sources, targets, held, sems = refs[:3], refs[3:6], refs[6:9], refs[9]
    loads = [pltpu.make_async_copy(a, b, sems.at[0, k]) for k, (a, b) in enumerate(zip(sources, held))]
    stores = [pltpu.make_async_copy(a, b, sems.at[1, k]) for k, (a, b) in enumerate(zip(held, targets))]
    for load in loads:
        load.start()
    for load, store in zip(loads, stores):
        load.wait()
        store.start()
    for store in stores:
        store.wait()


def local(
    lon_size, fields, cotangent, norm_gain, inner_weight, outer_weight, bias_table, merge_gain,
    merge_weight, split_weight,
):
    D = fields.shape[-1]
    to_quarter, to_pair, pair_of_quarter, dense, pick = (jnp.asarray(a) for a in orders())
    vmem = pl.BlockSpec(memory_space=pltpu.VMEM)
    hbm = pl.BlockSpec(memory_space=pltpu.HBM)
    operands = (
        split_weight, merge_weight, fields.transpose(1, 2, 0, 3), to_quarter,
        cotangent.transpose(1, 2, 0, 3), to_pair, norm_gain.reshape(1, D), inner_weight, bias_table,
        pick, outer_weight, pair_of_quarter, merge_gain.reshape(1, 4 * D), dense,
    )
    MS, CW = D // 2, 3 * D // lon_size

    def buf(*shape, dtype=BF16):
        return pltpu.VMEM(shape, dtype)

    quarters = (4, QUAD, D)
    wide = (lon_size, QUAD, 4 * D)
    scratch = [
        buf(WIN, D), buf(*quarters), buf(*quarters), buf(*wide), buf(*wide),
        buf(Z, 16, MS), buf(64, MS, dtype=F32), buf(Y, XH, 8, 2 * Z, MS),
        buf(Y, Z, XH, 16, MS),
        buf(*quarters), buf(*quarters), buf(*wide), buf(*quarters), buf(*quarters),
        buf(*quarters), buf(*quarters), buf(HEADS, ROWS, ROWS, dtype=F32), buf(ROWS, 3 * D),
        buf(ROWS, D),
        buf(lon_size, WIN, D), buf(ROWS, 3 * D), buf(lon_size, WIN, CW), buf(lon_size, WIN, CW),
        buf(Y * XH, 4 * Z, CW), buf(Y * XH, 4 * Z, CW), buf(Z, 16, CW // 3), buf(Z, 16, CW // 3),
        buf(*wide), buf(ROWS, D, dtype=F32), buf(HEADS, ROWS, ROWS, dtype=F32),
        buf(HEADS, 2 * SPAN, dtype=F32), buf(WIN, CW),
        buf(2, QUAD, 4 * D), buf(2, QUAD, 4 * D), buf(2, QUAD, 4 * D), buf(2, QUAD, 4 * D),
    ]
    count = 64
    scratch += [
        pltpu.SemaphoreType.DMA((count,)), pltpu.SemaphoreType.DMA((count,)),
        pltpu.SemaphoreType.DMA((3, Z)), pltpu.SemaphoreType.DMA((3, Z)),
        pltpu.SemaphoreType.DMA((len(operands),)),
        buf(WIN_LAT, WIN_LON, LEVELS, D), buf(WIN_LAT, WIN_LON, LEVELS, D),
        pltpu.SemaphoreType.DMA((2,)),
    ]
    scratch += [pltpu.VMEM(x.shape, x.dtype) for x in operands]
    grid_shape = (WIN_LAT, WIN_LON, LEVELS, D)
    out, grad, sums = pl.pallas_call(
        functools.partial(main_kernel, lon_size),
        out_shape=(
            jax.ShapeDtypeStruct(grid_shape, BF16),
            jax.ShapeDtypeStruct(grid_shape, BF16),
            jax.ShapeDtypeStruct((4, CW), F32),
        ),
        in_specs=[hbm] * len(operands),
        out_specs=(hbm, hbm, vmem),
        scratch_shapes=scratch,
        compiler_params=pltpu.CompilerParams(
            collective_id=0, has_side_effects=True, vmem_limit_bytes=63 * 1024 * 1024
        ),
    )(
        *operands,
    )
    results = (out, grad, sums)
    out, grad, sums = pl.pallas_call(
        settle_kernel,
        out_shape=tuple(jax.ShapeDtypeStruct(x.shape, x.dtype) for x in results),
        in_specs=[hbm] * 3,
        out_specs=(hbm,) * 3,
        scratch_shapes=[
            *(pltpu.VMEM(x.shape, x.dtype) for x in results),
            pltpu.SemaphoreType.DMA((2, 3)),
        ],
        compiler_params=pltpu.CompilerParams(vmem_limit_bytes=63 * 1024 * 1024),
    )(*results)
    return out.transpose(2, 0, 1, 3), grad.transpose(2, 0, 1, 3), sums


def solution(mesh):
    return jax.shard_map(
        functools.partial(local, mesh.shape["lon"]),
        mesh=mesh,
        in_specs=(
            P(None, "lat", "lon", None),
            P(None, "lat", "lon", None),
            P(),
            P(),
            P(),
            P(),
            P(),
            P("lat", None),
            P("lat", None),
        ),
        out_specs=(P(None, "lat", "lon", None), P(None, "lat", "lon", None), P("lat", "lon")),
        check_vma=False,
    )
```

```python
import functools
import math

import jax
import jax.numpy as jnp
import ml_dtypes
import numpy as np
from jax import lax
from jax.experimental import pallas as pl
from jax.experimental.pallas import tpu as pltpu
from jax.sharding import PartitionSpec as P

LEVELS = 2
WIN_LAT = 6
WIN_LON = 12
HEADS = 8
RELS = 759
SPAN = 384
QUAD = 48
ROWS = 4 * QUAD
WIN = 144
FAR = -1e30
Y, Z, XH = 4, 16, 2
FIRST = (6, -6, 3, -3, 8, 1, -1)
Z_FAR_FIRST = sorted(range(1, Z), key=lambda d: -min(d, Z - d))
SECOND = ((-1, 1), (1, -1), (-3, 1), (3, -1), (6, 1), (-6, -1), (-6, 1), (6, -1))
MESH = pl.DeviceIdType.MESH
NT = (((1,), (1,)), ((), ()))
TN = (((0,), (0,)), ((), ()))
F32 = jnp.float32
BF16 = jnp.bfloat16


def dot(a, b, dims=(((1,), (0,)), ((), ()))):
    return lax.dot_general(a, b, dims, preferred_element_type=F32)


def orders():
    natural, quarter, pair = {}, {}, {}
    base, compact = {}, {}
    for l in range(LEVELS):
        for r in range(WIN_LAT):
            for c in range(WIN_LON):
                token = (l, r, c)
                natural[token] = (r * WIN_LON + c) * LEVELS + l
                inside = (l * 3 + r % 3) * 6 + c % 6
                quarter[token] = ((r // 3) * 2 + c // 6) * QUAD + inside
                compact[token] = ((r // 3) * 2 + c // 6) * 36 + inside
                pair[token] = ((r % 2) * 2 + c % 2) * QUAD + (l * 3 + r // 2) * 6 + c // 2
                base[token] = (l * (2 * WIN_LAT - 1) + r) * (2 * WIN_LON - 1) + c
    to_quarter = np.zeros((ROWS, WIN), ml_dtypes.bfloat16)
    to_pair = np.zeros((ROWS, WIN), ml_dtypes.bfloat16)
    pair_of_quarter = np.zeros((ROWS, ROWS), ml_dtypes.bfloat16)
    dense = np.zeros((WIN, ROWS), ml_dtypes.bfloat16)
    pick = np.zeros((ROWS, SPAN), ml_dtypes.bfloat16)
    for token in natural:
        to_quarter[quarter[token], natural[token]] = 1
        to_pair[pair[token], natural[token]] = 1
        pair_of_quarter[pair[token], quarter[token]] = 1
        dense[compact[token], quarter[token]] = 1
        pick[quarter[token], base[token]] = 1
    return to_quarter, to_pair, pair_of_quarter, dense, pick


def make_bias(table_ref, padded_ref, pick, bias_ref):
    middle = (RELS - 1) // 2
    padded_ref[...] = jnp.zeros((HEADS, 2 * SPAN), F32)
    padded_ref[:, :RELS] = table_ref[...]
    back = 2 * SPAN - middle
    padded_ref[...] = pltpu.roll(padded_ref[...], back % 128, 1)
    used = jnp.sum(dot(jnp.ones((8, SPAN), BF16), pick, NT), axis=0, keepdims=True) > 0.5
    for h in range(HEADS):
        row = jnp.broadcast_to(padded_ref[h : h + 1, :], (SPAN, 2 * SPAN))
        shifted = pltpu.roll(row, back // 128 * 128, 1, stride=1, stride_axis=0)[:, :SPAN]
        high = shifted.astype(BF16)
        rest = shifted - high.astype(F32)
        middle_part = rest.astype(BF16)
        low = (rest - middle_part.astype(F32)).astype(BF16)
        total = jnp.zeros((ROWS, ROWS), F32)
        for part in (low, middle_part, high):
            total = total + dot(dot(pick, part, NT).astype(BF16), pick, NT)
        bias_ref[h] = jnp.where(used, total, FAR)


def norm_parts(values):
    mean = jnp.mean(values, axis=-1, keepdims=True)
    centred = values - mean
    variance = jnp.mean(centred * centred, axis=-1, keepdims=True)
    scale = lax.rsqrt(variance + 1e-05)
    return centred * scale, scale


def norm_back(unit, scale, grad, gain):
    g = grad * gain
    middle = jnp.mean(g, axis=-1, keepdims=True)
    along = jnp.mean(g * unit, axis=-1, keepdims=True)
    return scale * (g - middle - unit * along)


def main_kernel(
    lon_size,
    *refs,
):
    operands, refs = refs[:14], refs[14:]
    (
        outputs_hbm, grad_fields_hbm, grad_inner,
        nat, quads, win, cot_all, norm_all, raw, stack, split_w, merge_w,
        y_out, y_in, gm_out, gy_out, gy_in, gf_out, gf_in, att, proj, normed,
        toks_all, gp, gp_out, gp_in, dw_out, dw_in, z_out, z_in, so_out, unit_keep,
        bias, padded, gp_mid, gm_mid, gm_far_out, gm_far_in, gm_sum, so_mid, cross_out, cross_in,
        ssem, rsem, zsend, zrecv, lsem, outputs, grad_fields, osem,
        *local_refs,
    ) = refs
    loads = [
        pltpu.make_async_copy(src, dst, lsem.at[k])
        for k, (src, dst) in enumerate(zip(operands, local_refs))
    ]
    for load in loads:
        load.start()
    (
        split_shard, merge_shard, fields, to_quarter, cotangent, to_pair, gain, inner, table,
        pick, outer, pair_of_quarter, merge_gain, dense,
    ) = local_refs
    loads = dict(zip(map(id, local_refs), loads))

    def ready(*wanted):
        for ref in wanted:
            loads[id(ref)].wait()

    D = fields.shape[-1]
    MS = D // 2
    CW = 3 * D // lon_size
    KB = 8
    HD2 = 2 * D // HEADS
    i, j = lax.axis_index("lat"), lax.axis_index("lon")
    lat_size = Y * Z * XH
    xh = lax.rem(i, XH)
    z = lax.rem(i // XH, Z)
    y = i // (XH * Z)
    other = lax.rem(xh + 1, XH)
    mate = j + 1 - 2 * lax.rem(j, 2)
    across = lax.rem(j + 2, lon_size)
    beyond = lax.rem(mate + 2, lon_size)

    def at(yy, zz, xx):
        return (yy * Z + zz) * XH + xx

    def lat_by(d):
        return lax.rem(i + d + lat_size, lat_size)

    def lon_by(d):
        return lax.rem(j + d + lon_size, lon_size)

    def y_by(d):
        return lax.rem(y + d + Y, Y)

    def z_by(d):
        return lax.rem(z + d, Z)

    sems = iter(range(ssem.shape[0]))
    sent = []

    def push(src, dst, lat, lon):
        k = next(sems)
        copy = pltpu.make_async_remote_copy(
            src_ref=src, dst_ref=dst, send_sem=ssem.at[k], recv_sem=rsem.at[k],
            device_id=(lat, lon), device_id_type=MESH,
        )
        copy.start()
        sent.append(copy)
        return copy

    def arrive(copies):
        for copy in copies:
            copy.wait_recv()

    partners = []
    for a, b in ((0, 1), (1, 0), (1, 1)):
        partners += [(lat_by(a), lon_by(b)), (lat_by(-a), lon_by(-b))]
    for d in range(1, lon_size):
        partners.append((i, lon_by(d)))
    plane = [(dy, dx) for dy in range(Y) for dx in range(XH) if dy or dx]
    for dy, dx in plane:
        partners.append((at(y_by(dy), z, lax.rem(xh + dx, XH)), j))
    barrier = pltpu.get_barrier_semaphore()
    partners = [(at(y, z_by(d), xh), j) for d in Z_FAR_FIRST] + partners
    for lat, lon in partners:
        pl.semaphore_signal(barrier, inc=1, device_id=(lat, lon), device_id_type=MESH)

    ready(split_shard, merge_shard)
    for k in range(KB):
        stack[8 * k : 8 * k + 8, :] = split_shard[:, MS * k : MS * (k + 1)].astype(F32)
    row = lax.broadcasted_iota(jnp.int32, (16, 64), 0)
    col = lax.broadcasted_iota(jnp.int32, (16, 64), 1)
    sel = (col == (row // 2) * 8 + 2 * j + row % 2).astype(F32).astype(BF16)
    raw[z] = dot(sel, stack[...].astype(BF16)).astype(BF16)
    own = lax.broadcasted_iota(jnp.int32, (1, MS), 1)
    place = ((own // (2 * Z * XH)) * Z + (own // 2) % Z) * XH + (own // (2 * Z)) % XH
    col = lax.broadcasted_iota(jnp.int32, (2 * D, MS), 0)
    sel = (col == 8 * place + 2 * j + own % 2).astype(F32).astype(BF16)
    merge_w[y, z, xh] = dot(merge_shard[...], sel).astype(BF16)

    pl.semaphore_wait(barrier, len(partners))

    def roll_in(src, dst):
        return [
            push(src.at[(1 - a) * 2 + 1 - b], dst.at[a * 2 + b], lat_by(-a), lon_by(-b))
            for a, b in ((1, 1), (1, 0), (0, 1))
        ]

    def roll_out(src, dst):
        return [
            push(src.at[a * 2 + b], dst.at[(1 - a) * 2 + 1 - b], lat_by(a), lon_by(b))
            for a, b in ((1, 1), (1, 0), (0, 1))
        ]

    def z_send(kind, slot, r, d):
        block, k = slot(z_by(r)), (r - d) % Z
        pltpu.make_async_remote_copy(
            src_ref=block, dst_ref=block, send_sem=zsend.at[kind, k], recv_sem=zrecv.at[kind, k],
            device_id=(at(y, z_by(d % Z), xh), j), device_id_type=MESH,
        ).start()

    def z_wait(kind, slot, steps, received=True):
        for e in steps:
            block, k = slot(z_by(e % Z)), e % Z
            copy = pltpu.make_async_remote_copy(
                src_ref=block, dst_ref=block, send_sem=zsend.at[kind, k], recv_sem=zrecv.at[kind, k],
                device_id=(at(y, z_by(1), xh), j), device_id_type=MESH,
            )
            if received:
                copy.wait_recv()
            else:
                copy.wait_send()

    def raw_slot(k):
        return raw.at[k]

    def merge_slot(k):
        return merge_w.at[y, k, xh]

    def z_first(kind, slot):
        for d in FIRST:
            z_send(kind, slot, 0, d)

    def z_second(kind, slot):
        z_wait(kind, slot, [-d for d in FIRST if abs(d) < Z // 2])
        for r, d in SECOND:
            z_send(kind, slot, r % Z, d)

    def z_third(kind, slot):
        z_wait(kind, slot, [e for e in range(1, Z) if e not in [-d % Z for d in FIRST if abs(d) < Z // 2]])

    def sums_z(d):
        return pltpu.make_async_remote_copy(
            src_ref=z_out.at[z_by(d)], dst_ref=z_in.at[z], send_sem=zsend.at[2, d], recv_sem=zrecv.at[2, d],
            device_id=(at(y, z_by(d), xh), j), device_id_type=MESH,
        )

    z_first(0, raw_slot)
    z_first(1, merge_slot)

    def to_natural(src):
        for r in range(WIN_LAT):
            for c in range(WIN_LON):
                start = (r * WIN_LON + c) * LEVELS
                nat[start : start + LEVELS, :] = src[r, c]
        return nat[...]

    ready(fields, to_quarter)
    quads[...] = dot(to_quarter[...], to_natural(fields)).astype(BF16).reshape(4, QUAD, D)
    win[0] = quads[3]
    fields_move = roll_in(quads, win)

    def gather_start(whole):
        mine = whole.at[j]
        return push(mine, mine, i, across), push(mine, mine, i, mate)

    def gather_relay(whole, started):
        arrive(started[:1])
        came = whole.at[across]
        return started[1], push(came, came, i, mate)

    def reduce_start(src, mid):
        return push(src.at[beyond], mid.at[1], i, mate), push(src.at[mate], mid.at[0], i, mate)

    def reduce_cross(src, mid, started, slot):
        arrive(started[:1])
        cross_out[slot] = (src[across].astype(F32) + mid[1].astype(F32)).astype(BF16)
        return [started[1], push(cross_out.at[slot], cross_in.at[slot], i, across)]

    def reduce_end(src, mid, crossed, slot):
        arrive(crossed)
        return src[j].astype(F32) + mid[0].astype(F32) + cross_in[slot].astype(F32)

    def lanes(rows):
        return jnp.concatenate([rows[QUAD * s : QUAD * (s + 1)] for s in range(4)], axis=1)

    def stacked(wide):
        return jnp.concatenate([wide[:, D * s : D * (s + 1)] for s in range(4)], axis=0)

    ready(cotangent, to_pair)
    cot_all[j] = lanes(dot(to_pair[...], to_natural(cotangent)).astype(BF16))

    ready(table, pick)
    make_bias(table, padded, pick[...], bias)
    z_second(0, raw_slot)
    z_second(1, merge_slot)
    arrive(fields_move)
    rolled = win[...].reshape(ROWS, D).astype(F32)
    ready(gain, inner)
    unit, scale = norm_parts(rolled)
    unit_keep[...] = unit
    normed[...] = (unit * gain[...]).astype(BF16)
    proj[...] = dot(normed[...], inner[...]).astype(BF16)

    full = Z * 16
    out = lax.broadcasted_iota(jnp.int32, (full, 1), 0)
    src = lax.broadcasted_iota(jnp.int32, (full, full), 1)
    want = ((out % (2 * Z)) // 2) * 16 + (out // (2 * Z)) * 2 + out % 2
    regroup = (src == want).astype(F32).astype(BF16)
    z_third(0, raw_slot)
    split_w[y, xh] = dot(regroup, raw[...].reshape(full, MS)).astype(BF16).reshape(KB, 2 * Z, MS)
    split_x = push(split_w.at[y, xh], split_w.at[y, xh], at(y, z, other), j)
    z_third(1, merge_slot)
    merge_x = push(merge_w.at[y, :, xh], merge_w.at[y, :, xh], at(y, z, other), j)

    def y_spread(whole):
        return [push(whole.at[y], whole.at[y], at(y_by(d), z, xh), j) for d in (1, -1)]

    arrive([split_x])
    split_y = y_spread(split_w)

    half_q = lax.broadcasted_iota(jnp.int32, (ROWS, 1), 0) // (2 * QUAD)
    half_k = lax.broadcasted_iota(jnp.int32, (1, ROWS), 1) // (2 * QUAD)
    allowed = jnp.logical_or(half_q == half_k, i != lat_size - 1)
    first = lax.broadcasted_iota(jnp.int32, (ROWS, HD2), 1) < HD2 // 2
    inv_root = (HD2 // 2) ** -0.5

    def of_head(values, h):
        return jnp.where(first if h % 2 == 0 else jnp.logical_not(first), values, jnp.zeros_like(values))

    def attend(pair):
        at_q = slice(HD2 * pair, HD2 * (pair + 1))
        at_k = slice(D + HD2 * pair, D + HD2 * (pair + 1))
        at_v = slice(2 * D + HD2 * pair, 2 * D + HD2 * (pair + 1))
        q, k, v = proj[:, at_q], proj[:, at_k], proj[:, at_v]
        results = []
        for h in (2 * pair, 2 * pair + 1):
            scores = dot(of_head(q, h), k, NT) * inv_root + bias[h]
            scores = jnp.where(allowed, scores, FAR)
            weights = jnp.exp(scores - jnp.max(scores, axis=-1, keepdims=True))
            weights = weights / jnp.sum(weights, axis=-1, keepdims=True)
            att[h] = weights
            results.append(dot(weights.astype(BF16), v))
        return jnp.where(first, results[0], results[1]).astype(BF16)

    attended = [attend(0), attend(1)]

    arrive([merge_x])
    merge_y = y_spread(merge_w)
    cot_move = gather_start(cot_all)

    attended += [attend(2), attend(3)]
    attended = jnp.concatenate(attended, axis=1)
    ready(outer)
    y_rolled = (rolled + dot(attended, outer[...])).astype(BF16)
    y_out[...] = y_rolled.reshape(4, QUAD, D)
    y_in[3] = y_out[0]
    y_move = roll_out(y_out, y_in)

    row = lax.broadcasted_iota(jnp.int32, (D, D), 0)
    col = lax.broadcasted_iota(jnp.int32, (1, D), 1)
    block = col // (4 * Z)
    want = ((block // XH) * Z + (col // 4) % Z) * (4 * XH) + (block % XH) * 4 + col % 4
    swap = (row == want).astype(F32).astype(BF16)
    ready(dense)
    toks = dot(dense[...], normed[...]).astype(BF16)
    toks_all[j] = dot(toks, swap).astype(BF16)


    def y_forward(whole, halves):
        return [
            push(halves(whole, y_by(-1), 0), halves(whole, y_by(-1), 0), at(y_by(1), z, xh), j),
            push(halves(whole, y_by(1), 1), halves(whole, y_by(1), 1), at(y_by(-1), z, xh), j),
        ]

    arrive(split_y)
    split_f = y_forward(split_w, lambda w, yy, part: w.at[yy, part])
    cot_rest = gather_relay(cot_all, cot_move)

    arrive(y_move)
    ready(pair_of_quarter, merge_gain)
    y_pairs = lanes(dot(pair_of_quarter[...], y_in[...].reshape(ROWS, D)))
    pair_unit, pair_scale = norm_parts(y_pairs)
    norm_all[j] = (pair_unit * merge_gain[...]).astype(BF16)
    norm_move = gather_start(norm_all)
    toks_move = gather_start(toks_all)

    arrive(merge_y)
    merge_f = y_forward(merge_w, lambda w, yy, part: w.at[yy, pl.ds(part * (Z // 2), Z // 2)])

    arrive(cot_rest)
    arrive(split_f)

    def split_block(k):
        return split_w[:, :, k].reshape(MS, MS)

    cots = cot_all[...].reshape(lon_size * QUAD, 4 * D)
    grad_merged = dot(cots[:, :MS], split_block(0), NT)
    for k in range(1, KB):
        grad_merged = grad_merged + dot(cots[:, MS * k : MS * (k + 1)], split_block(k), NT)
    grad_merged = grad_merged.astype(BF16)
    near = (0, 1, -1, 2)

    def gm_part(first, count):
        for k in range(first, first + count):
            block = merge_w[y_by(near[k])].reshape(D, MS)
            gm_out[:, k] = dot(grad_merged, block, NT).astype(BF16).reshape(lon_size, QUAD, D)
        part = pl.ds(first, count)
        there = push(gm_out.at[beyond, part], gm_mid.at[1, part], i, mate)
        here = push(gm_out.at[mate, part], gm_mid.at[0, part], i, mate)
        arrive([there])
        pair = gm_out[across, part].astype(F32) + gm_mid[1, part].astype(F32)
        gm_far_out[part] = pair.astype(BF16)
        return [here, push(gm_far_out.at[part], gm_far_in.at[part], i, across)]

    gm_moves = gm_part(0, 3)
    arrive(merge_f)
    gm_moves += gm_part(3, 1)
    merge_full = merge_w[...].reshape(4 * D, MS)
    norm_rest = gather_relay(norm_all, norm_move)
    toks_rest = gather_relay(toks_all, toks_move)

    arrive(gm_moves)
    for k in range(4):
        found = gm_out[j, k].astype(F32) + gm_mid[0, k].astype(F32) + gm_far_in[k].astype(F32)
        gm_sum[y_by(near[k])] = found
    grad_mnorm = jnp.concatenate([gm_sum[k] for k in range(4)], axis=1)
    grad_y = cot_all[j].astype(F32) + norm_back(pair_unit, pair_scale, grad_mnorm, merge_gain[...])
    grad_y = dot(pair_of_quarter[...], stacked(grad_y.astype(BF16)), TN).astype(BF16)
    gy_out[...] = grad_y.reshape(4, QUAD, D)
    gy_in[0] = gy_out[3]
    gy_move = roll_in(gy_out, gy_in)

    arrive(norm_rest)
    merged = dot(norm_all[...].reshape(lon_size * QUAD, 4 * D), merge_full).astype(BF16)
    for k in range(KB):
        part = dot(merged, split_block(k)).astype(BF16)
        so_out[:, :, MS * k : MS * (k + 1)] = part.reshape(lon_size, QUAD, MS)
    so_start = reduce_start(so_out, so_mid)

    arrive(gy_move)
    so_crossed = reduce_cross(so_out, so_mid, so_start, 1)
    grad_rolled_y = gy_in[...].reshape(ROWS, D)
    grad_attended = dot(grad_rolled_y, outer[...], NT).astype(BF16)
    for pair in range(HEADS // 2):
        at_q = slice(HD2 * pair, HD2 * (pair + 1))
        at_k = slice(D + HD2 * pair, D + HD2 * (pair + 1))
        at_v = slice(2 * D + HD2 * pair, 2 * D + HD2 * (pair + 1))
        q, k, v = proj[:, at_q], proj[:, at_k], proj[:, at_v]
        g = grad_attended[:, at_q]
        found = []
        for h in (2 * pair, 2 * pair + 1):
            weights = att[h]
            grad_p = dot(of_head(g, h), v, NT)
            grad_v = dot(weights.astype(BF16), g, TN)
            shared = jnp.sum(weights * grad_p, axis=-1, keepdims=True)
            grad_s = (weights * (grad_p - shared)).astype(BF16)
            found.append((dot(grad_s, k) * inv_root, dot(grad_s, q, TN) * inv_root, grad_v))
        for where, even, odd in zip((at_q, at_k, at_v), *found):
            gp[:, where] = jnp.where(first, even, odd).astype(BF16)
    few = dot(dense[...], gp[...]).astype(BF16)
    for d in range(lon_size):
        gp_out[d] = few[:, CW * d : CW * (d + 1)]
    gp_far = push(gp_out.at[beyond], gp_mid, i, across)
    gp_move = [
        push(gp_out.at[across], gp_in.at[j], i, across),
        push(gp_out.at[mate], gp_in.at[j], i, mate),
    ]
    gp_in[j] = gp_out[j]

    grad_normed = dot(gp[...], inner[...], NT)
    grad_in = grad_rolled_y.astype(F32) + norm_back(unit_keep[...], scale, grad_normed, gain[...])
    gf_out[...] = grad_in.astype(BF16).reshape(4, QUAD, D)
    gf_in[3] = gf_out[0]
    gf_move = roll_out(gf_out, gf_in)

    arrive([gp_far])
    gp_move.append(push(gp_mid, gp_in.at[across], i, mate))

    arrive(toks_rest)
    arrive(gp_move[:2])
    summed = dot(toks_all[j], gp_in[j], TN) + dot(toks_all[mate], gp_in[mate], TN)
    summed = summed + dot(toks_all[across], gp_in[across], TN)
    arrive(gp_move[2:])
    summed = summed + dot(toks_all[beyond], gp_in[beyond], TN)
    dw_out[...] = summed.astype(BF16).reshape(Y * XH, 4 * Z, CW)
    dw_move = []
    for dy, dx in sorted(plane, key=lambda p: -min(p[0], Y - p[0]) - 2 * p[1]):
        yy, xx = y_by(dy), lax.rem(xh + dx, XH)
        dw_move.append(push(dw_out.at[yy * XH + xx], dw_in.at[y * XH + xh], at(yy, z, xx), j))

    def from_pairs(wide):
        return dot(to_pair[...], stacked(wide), TN).astype(BF16)

    def put(dst, rows):
        for r in range(WIN_LAT):
            for c in range(WIN_LON):
                start = (r * WIN_LON + c) * LEVELS
                dst[r, c] = rows[start : start + LEVELS]

    arrive(dw_move)
    mine = dw_out[y * XH + xh].astype(F32)
    for dy, dx in plane:
        slot = y_by(-dy) * XH + lax.rem(xh + dx, XH)
        mine = mine + dw_in[slot].astype(F32)
    mine = mine.astype(BF16)
    CB = CW // 3
    tall = jnp.concatenate([mine[:, CB * c : CB * (c + 1)] for c in range(3)], axis=0)
    row = lax.broadcasted_iota(jnp.int32, (16 * Z, 1), 0)
    col = lax.broadcasted_iota(jnp.int32, (16 * Z, 12 * Z), 1)
    inner_row = row % 16
    want = (inner_row // 4) * (4 * Z) + (row // 16) * 4 + inner_row % 4
    spread = jnp.logical_and(col == want, inner_row < 12).astype(F32).astype(BF16)
    z_out[...] = dot(spread, tall).astype(BF16).reshape(Z, 16, CB)

    for d in Z_FAR_FIRST:
        sums_z(d).start()
    z_in[z] = z_out[z]

    split_out = reduce_end(so_out, so_mid, so_crossed, 1)
    put(outputs, from_pairs((y_pairs + split_out).astype(BF16)))
    stores = [pltpu.make_async_copy(outputs, outputs_hbm, osem.at[0])]
    stores[0].start()

    arrive(gf_move)
    put(grad_fields, dot(to_quarter[...], gf_in[...].reshape(ROWS, D), TN).astype(BF16))
    stores.append(pltpu.make_async_copy(grad_fields, grad_fields_hbm, osem.at[1]))
    stores[1].start()

    @pl.loop(1, Z)
    def _(d):
        sums_z(d).wait_recv()

    owned = jnp.sum(z_in[...].astype(F32), axis=0)
    shrink = 1.0 / math.sqrt(WIN * lat_size * lon_size)
    for c in range(3):
        grad_inner[:, CB * c : CB * (c + 1)] = owned[4 * c : 4 * c + 4] * shrink

    for store in stores:
        store.wait()
    for copy in sent:
        copy.wait_send()

    @pl.loop(1, Z)
    def _(d):
        sums_z(d).wait_send()

    for kind, slot in enumerate((raw_slot, merge_slot)):
        z_wait(kind, slot, range(1, Z), received=False)


def settle_kernel(*refs):
    sources, targets, held, sems = refs[:3], refs[3:6], refs[6:9], refs[9]
    loads = [pltpu.make_async_copy(a, b, sems.at[0, k]) for k, (a, b) in enumerate(zip(sources, held))]
    stores = [pltpu.make_async_copy(a, b, sems.at[1, k]) for k, (a, b) in enumerate(zip(held, targets))]
    for load in loads:
        load.start()
    for load, store in zip(loads, stores):
        load.wait()
        store.start()
    for store in stores:
        store.wait()


def local(
    lon_size, fields, cotangent, norm_gain, inner_weight, outer_weight, bias_table, merge_gain,
    merge_weight, split_weight,
):
    D = fields.shape[-1]
    to_quarter, to_pair, pair_of_quarter, dense, pick = (jnp.asarray(a) for a in orders())
    vmem = pl.BlockSpec(memory_space=pltpu.VMEM)
    hbm = pl.BlockSpec(memory_space=pltpu.HBM)
    operands = (
        split_weight, merge_weight, fields.transpose(1, 2, 0, 3), to_quarter,
        cotangent.transpose(1, 2, 0, 3), to_pair, norm_gain.reshape(1, D), inner_weight, bias_table,
        pick, outer_weight, pair_of_quarter, merge_gain.reshape(1, 4 * D), dense,
    )
    MS, CW = D // 2, 3 * D // lon_size

    def buf(*shape, dtype=BF16):
        return pltpu.VMEM(shape, dtype)

    quarters = (4, QUAD, D)
    wide = (lon_size, QUAD, 4 * D)
    scratch = [
        buf(WIN, D), buf(*quarters), buf(*quarters), buf(*wide), buf(*wide),
        buf(Z, 16, MS), buf(64, MS, dtype=F32), buf(Y, XH, 8, 2 * Z, MS),
        buf(Y, Z, XH, 16, MS),
        buf(*quarters), buf(*quarters), buf(lon_size, 4, QUAD, D), buf(*quarters), buf(*quarters),
        buf(*quarters), buf(*quarters), buf(HEADS, ROWS, ROWS, dtype=F32), buf(ROWS, 3 * D),
        buf(ROWS, D),
        buf(lon_size, WIN, D), buf(ROWS, 3 * D), buf(lon_size, WIN, CW), buf(lon_size, WIN, CW),
        buf(Y * XH, 4 * Z, CW), buf(Y * XH, 4 * Z, CW), buf(Z, 16, CW // 3), buf(Z, 16, CW // 3),
        buf(*wide), buf(ROWS, D, dtype=F32), buf(HEADS, ROWS, ROWS, dtype=F32),
        buf(HEADS, 2 * SPAN, dtype=F32), buf(WIN, CW),
        buf(2, 4, QUAD, D), buf(4, QUAD, D), buf(4, QUAD, D), buf(4, QUAD, D, dtype=F32),
        buf(2, QUAD, 4 * D), buf(2, QUAD, 4 * D), buf(2, QUAD, 4 * D),
    ]
    count = 64
    scratch += [
        pltpu.SemaphoreType.DMA((count,)), pltpu.SemaphoreType.DMA((count,)),
        pltpu.SemaphoreType.DMA((3, Z)), pltpu.SemaphoreType.DMA((3, Z)),
        pltpu.SemaphoreType.DMA((len(operands),)),
        buf(WIN_LAT, WIN_LON, LEVELS, D), buf(WIN_LAT, WIN_LON, LEVELS, D),
        pltpu.SemaphoreType.DMA((2,)),
    ]
    scratch += [pltpu.VMEM(x.shape, x.dtype) for x in operands]
    grid_shape = (WIN_LAT, WIN_LON, LEVELS, D)
    out, grad, sums = pl.pallas_call(
        functools.partial(main_kernel, lon_size),
        out_shape=(
            jax.ShapeDtypeStruct(grid_shape, BF16),
            jax.ShapeDtypeStruct(grid_shape, BF16),
            jax.ShapeDtypeStruct((4, CW), F32),
        ),
        in_specs=[hbm] * len(operands),
        out_specs=(hbm, hbm, vmem),
        scratch_shapes=scratch,
        compiler_params=pltpu.CompilerParams(
            collective_id=0, has_side_effects=True, vmem_limit_bytes=63 * 1024 * 1024
        ),
    )(
        *operands,
    )
    results = (out, grad, sums)
    out, grad, sums = pl.pallas_call(
        settle_kernel,
        out_shape=tuple(jax.ShapeDtypeStruct(x.shape, x.dtype) for x in results),
        in_specs=[hbm] * 3,
        out_specs=(hbm,) * 3,
        scratch_shapes=[
            *(pltpu.VMEM(x.shape, x.dtype) for x in results),
            pltpu.SemaphoreType.DMA((2, 3)),
        ],
        compiler_params=pltpu.CompilerParams(vmem_limit_bytes=63 * 1024 * 1024),
    )(*results)
    return out.transpose(2, 0, 1, 3), grad.transpose(2, 0, 1, 3), sums


def solution(mesh):
    return jax.shard_map(
        functools.partial(local, mesh.shape["lon"]),
        mesh=mesh,
        in_specs=(
            P(None, "lat", "lon", None),
            P(None, "lat", "lon", None),
            P(),
            P(),
            P(),
            P(),
            P(),
            P("lat", None),
            P("lat", None),
        ),
        out_specs=(P(None, "lat", "lon", None), P(None, "lat", "lon", None), P("lat", "lon")),
        check_vma=False,
    )
```

```python
import functools
import math

import jax
import jax.numpy as jnp
import ml_dtypes
import numpy as np
from jax import lax
from jax.experimental import pallas as pl
from jax.experimental.pallas import tpu as pltpu
from jax.sharding import PartitionSpec as P

LEVELS = 2
WIN_LAT = 6
WIN_LON = 12
HEADS = 8
RELS = 759
SPAN = 384
QUAD = 48
ROWS = 4 * QUAD
WIN = 144
FAR = -1e30
Y, Z, XH = 4, 16, 2
FIRST = (6, -6, 3, -3, 8, 1, -1)
Z_FAR_FIRST = sorted(range(1, Z), key=lambda d: -min(d, Z - d))
SECOND = ((-1, 1), (1, -1), (-3, 1), (3, -1), (6, 1), (-6, -1), (-6, 1), (6, -1))
MESH = pl.DeviceIdType.MESH
NT = (((1,), (1,)), ((), ()))
TN = (((0,), (0,)), ((), ()))
F32 = jnp.float32
BF16 = jnp.bfloat16


def dot(a, b, dims=(((1,), (0,)), ((), ()))):
    return lax.dot_general(a, b, dims, preferred_element_type=F32)


def orders():
    natural, quarter, pair = {}, {}, {}
    base, compact = {}, {}
    for l in range(LEVELS):
        for r in range(WIN_LAT):
            for c in range(WIN_LON):
                token = (l, r, c)
                natural[token] = (r * WIN_LON + c) * LEVELS + l
                inside = (l * 3 + r % 3) * 6 + c % 6
                quarter[token] = ((r // 3) * 2 + c // 6) * QUAD + inside
                compact[token] = ((r // 3) * 2 + c // 6) * 36 + inside
                pair[token] = ((r % 2) * 2 + c % 2) * QUAD + (l * 3 + r // 2) * 6 + c // 2
                base[token] = (l * (2 * WIN_LAT - 1) + r) * (2 * WIN_LON - 1) + c
    to_quarter = np.zeros((ROWS, WIN), ml_dtypes.bfloat16)
    to_pair = np.zeros((ROWS, WIN), ml_dtypes.bfloat16)
    pair_of_quarter = np.zeros((ROWS, ROWS), ml_dtypes.bfloat16)
    dense = np.zeros((WIN, ROWS), ml_dtypes.bfloat16)
    pick = np.zeros((ROWS, SPAN), ml_dtypes.bfloat16)
    for token in natural:
        to_quarter[quarter[token], natural[token]] = 1
        to_pair[pair[token], natural[token]] = 1
        pair_of_quarter[pair[token], quarter[token]] = 1
        dense[compact[token], quarter[token]] = 1
        pick[quarter[token], base[token]] = 1
    return to_quarter, to_pair, pair_of_quarter, dense, pick


def make_bias(table_ref, padded_ref, pick, bias_ref):
    middle = (RELS - 1) // 2
    padded_ref[...] = jnp.zeros((HEADS, 2 * SPAN), F32)
    padded_ref[:, :RELS] = table_ref[...]
    back = 2 * SPAN - middle
    padded_ref[...] = pltpu.roll(padded_ref[...], back % 128, 1)
    used = jnp.sum(dot(jnp.ones((8, SPAN), BF16), pick, NT), axis=0, keepdims=True) > 0.5
    for h in range(HEADS):
        row = jnp.broadcast_to(padded_ref[h : h + 1, :], (SPAN, 2 * SPAN))
        shifted = pltpu.roll(row, back // 128 * 128, 1, stride=1, stride_axis=0)[:, :SPAN]
        high = shifted.astype(BF16)
        rest = shifted - high.astype(F32)
        middle_part = rest.astype(BF16)
        low = (rest - middle_part.astype(F32)).astype(BF16)
        total = jnp.zeros((ROWS, ROWS), F32)
        for part in (low, middle_part, high):
            total = total + dot(dot(pick, part, NT).astype(BF16), pick, NT)
        bias_ref[h] = jnp.where(used, total, FAR)


def norm_parts(values):
    mean = jnp.mean(values, axis=-1, keepdims=True)
    centred = values - mean
    variance = jnp.mean(centred * centred, axis=-1, keepdims=True)
    scale = lax.rsqrt(variance + 1e-05)
    return centred * scale, scale


def norm_back(unit, scale, grad, gain):
    g = grad * gain
    middle = jnp.mean(g, axis=-1, keepdims=True)
    along = jnp.mean(g * unit, axis=-1, keepdims=True)
    return scale * (g - middle - unit * along)


def main_kernel(
    lon_size,
    *refs,
):
    operands, refs = refs[:14], refs[14:]
    (
        outputs_hbm, grad_fields_hbm, grad_inner,
        nat, quads, win, cot_all, norm_all, raw, stack, split_w, merge_w,
        y_out, y_in, gm_out, gy_out, gy_in, gf_out, gf_in, att, proj, normed,
        toks_all, gp, gp_out, gp_in, dw_out, dw_in, z_out, z_in, so_out, unit_keep,
        bias, padded, gp_mid, gm_mid, gm_far_out, gm_far_in, gm_sum, so_mid, cross_out, cross_in,
        ssem, rsem, zsend, zrecv, lsem, outputs, grad_fields, osem,
        *local_refs,
    ) = refs
    loads = [
        pltpu.make_async_copy(src, dst, lsem.at[k])
        for k, (src, dst) in enumerate(zip(operands, local_refs))
    ]
    for load in loads:
        load.start()
    (
        split_shard, merge_shard, fields, to_quarter, cotangent, to_pair, gain, inner, table,
        pick, outer, pair_of_quarter, merge_gain, dense,
    ) = local_refs
    loads = dict(zip(map(id, local_refs), loads))

    def ready(*wanted):
        for ref in wanted:
            loads[id(ref)].wait()

    D = fields.shape[-1]
    MS = D // 2
    CW = 3 * D // lon_size
    KB = 8
    HD2 = 2 * D // HEADS
    i, j = lax.axis_index("lat"), lax.axis_index("lon")
    lat_size = Y * Z * XH
    xh = lax.rem(i, XH)
    z = lax.rem(i // XH, Z)
    y = i // (XH * Z)
    other = lax.rem(xh + 1, XH)
    mate = j + 1 - 2 * lax.rem(j, 2)
    across = lax.rem(j + 2, lon_size)
    beyond = lax.rem(mate + 2, lon_size)

    def at(yy, zz, xx):
        return (yy * Z + zz) * XH + xx

    def lat_by(d):
        return lax.rem(i + d + lat_size, lat_size)

    def lon_by(d):
        return lax.rem(j + d + lon_size, lon_size)

    def y_by(d):
        return lax.rem(y + d + Y, Y)

    def z_by(d):
        return lax.rem(z + d, Z)

    sems = iter(range(ssem.shape[0]))
    sent = []

    def push(src, dst, lat, lon):
        k = next(sems)
        copy = pltpu.make_async_remote_copy(
            src_ref=src, dst_ref=dst, send_sem=ssem.at[k], recv_sem=rsem.at[k],
            device_id=(lat, lon), device_id_type=MESH,
        )
        copy.start()
        sent.append(copy)
        return copy

    def arrive(copies):
        for copy in copies:
            copy.wait_recv()

    partners = []
    for a, b in ((0, 1), (1, 0), (1, 1)):
        partners += [(lat_by(a), lon_by(b)), (lat_by(-a), lon_by(-b))]
    for d in range(1, lon_size):
        partners.append((i, lon_by(d)))
    plane = [(dy, dx) for dy in range(Y) for dx in range(XH) if dy or dx]
    for dy, dx in plane:
        partners.append((at(y_by(dy), z, lax.rem(xh + dx, XH)), j))
    barrier = pltpu.get_barrier_semaphore()
    partners = [(at(y, z_by(d), xh), j) for d in Z_FAR_FIRST] + partners
    for lat, lon in partners:
        pl.semaphore_signal(barrier, inc=1, device_id=(lat, lon), device_id_type=MESH)

    ready(split_shard, merge_shard)
    for k in range(KB):
        stack[8 * k : 8 * k + 8, :] = split_shard[:, MS * k : MS * (k + 1)].astype(F32)
    row = lax.broadcasted_iota(jnp.int32, (16, 64), 0)
    col = lax.broadcasted_iota(jnp.int32, (16, 64), 1)
    sel = (col == (row // 2) * 8 + 2 * j + row % 2).astype(F32).astype(BF16)
    raw[z] = dot(sel, stack[...].astype(BF16)).astype(BF16)
    own = lax.broadcasted_iota(jnp.int32, (1, MS), 1)
    place = ((own // (2 * Z * XH)) * Z + (own // 2) % Z) * XH + (own // (2 * Z)) % XH
    col = lax.broadcasted_iota(jnp.int32, (2 * D, MS), 0)
    sel = (col == 8 * place + 2 * j + own % 2).astype(F32).astype(BF16)
    merge_w[y, z, xh] = dot(merge_shard[...], sel).astype(BF16)

    pl.semaphore_wait(barrier, len(partners))

    def roll_in(src, dst):
        return [
            push(src.at[(1 - a) * 2 + 1 - b], dst.at[a * 2 + b], lat_by(-a), lon_by(-b))
            for a, b in ((1, 1), (1, 0), (0, 1))
        ]

    def roll_out(src, dst):
        return [
            push(src.at[a * 2 + b], dst.at[(1 - a) * 2 + 1 - b], lat_by(a), lon_by(b))
            for a, b in ((1, 1), (1, 0), (0, 1))
        ]

    def z_send(kind, slot, r, d):
        block, k = slot(z_by(r)), (r - d) % Z
        pltpu.make_async_remote_copy(
            src_ref=block, dst_ref=block, send_sem=zsend.at[kind, k], recv_sem=zrecv.at[kind, k],
            device_id=(at(y, z_by(d % Z), xh), j), device_id_type=MESH,
        ).start()

    def z_wait(kind, slot, steps, received=True):
        for e in steps:
            block, k = slot(z_by(e % Z)), e % Z
            copy = pltpu.make_async_remote_copy(
                src_ref=block, dst_ref=block, send_sem=zsend.at[kind, k], recv_sem=zrecv.at[kind, k],
                device_id=(at(y, z_by(1), xh), j), device_id_type=MESH,
            )
            if received:
                copy.wait_recv()
            else:
                copy.wait_send()

    def raw_slot(k):
        return raw.at[k]

    def merge_slot(k):
        return merge_w.at[y, k, xh]

    def z_first(kind, slot):
        for d in FIRST:
            z_send(kind, slot, 0, d)

    def z_second(kind, slot):
        z_wait(kind, slot, [-d for d in FIRST if abs(d) < Z // 2])
        for r, d in SECOND:
            z_send(kind, slot, r % Z, d)

    def z_third(kind, slot):
        z_wait(kind, slot, [e for e in range(1, Z) if e not in [-d % Z for d in FIRST if abs(d) < Z // 2]])

    def sums_z(d):
        return pltpu.make_async_remote_copy(
            src_ref=z_out.at[z_by(d)], dst_ref=z_in.at[z], send_sem=zsend.at[2, d], recv_sem=zrecv.at[2, d],
            device_id=(at(y, z_by(d), xh), j), device_id_type=MESH,
        )

    z_first(0, raw_slot)
    z_first(1, merge_slot)

    def to_natural(src):
        for r in range(WIN_LAT):
            for c in range(WIN_LON):
                start = (r * WIN_LON + c) * LEVELS
                nat[start : start + LEVELS, :] = src[r, c]
        return nat[...]

    ready(fields, to_quarter)
    quads[...] = dot(to_quarter[...], to_natural(fields)).astype(BF16).reshape(4, QUAD, D)
    win[0] = quads[3]
    fields_move = roll_in(quads, win)

    def gather_start(whole):
        mine = whole.at[j]
        return push(mine, mine, i, across), push(mine, mine, i, mate)

    def gather_relay(whole, started):
        arrive(started[:1])
        came = whole.at[across]
        return started[1], push(came, came, i, mate)

    def reduce_start(src, mid):
        return push(src.at[beyond], mid.at[1], i, mate), push(src.at[mate], mid.at[0], i, mate)

    def reduce_cross(src, mid, started, slot):
        arrive(started[:1])
        cross_out[slot] = (src[across].astype(F32) + mid[1].astype(F32)).astype(BF16)
        return [started[1], push(cross_out.at[slot], cross_in.at[slot], i, across)]

    def reduce_end(src, mid, crossed, slot):
        arrive(crossed)
        return src[j].astype(F32) + mid[0].astype(F32) + cross_in[slot].astype(F32)

    def lanes(rows):
        return jnp.concatenate([rows[QUAD * s : QUAD * (s + 1)] for s in range(4)], axis=1)

    def stacked(wide):
        return jnp.concatenate([wide[:, D * s : D * (s + 1)] for s in range(4)], axis=0)

    ready(cotangent, to_pair)
    cot_all[j] = lanes(dot(to_pair[...], to_natural(cotangent)).astype(BF16))

    ready(table, pick)
    make_bias(table, padded, pick[...], bias)
    z_second(0, raw_slot)
    z_second(1, merge_slot)
    arrive(fields_move)
    rolled = win[...].reshape(ROWS, D).astype(F32)
    ready(gain, inner)
    unit, scale = norm_parts(rolled)
    unit_keep[...] = unit
    normed[...] = (unit * gain[...]).astype(BF16)
    proj[...] = dot(normed[...], inner[...]).astype(BF16)

    full = Z * 16
    out = lax.broadcasted_iota(jnp.int32, (full, 1), 0)
    src = lax.broadcasted_iota(jnp.int32, (full, full), 1)
    want = ((out % (2 * Z)) // 2) * 16 + (out // (2 * Z)) * 2 + out % 2
    regroup = (src == want).astype(F32).astype(BF16)
    z_third(0, raw_slot)
    split_w[y, xh] = dot(regroup, raw[...].reshape(full, MS)).astype(BF16).reshape(KB, 2 * Z, MS)
    split_x = push(split_w.at[y, xh], split_w.at[y, xh], at(y, z, other), j)
    z_third(1, merge_slot)
    merge_x = push(merge_w.at[y, :, xh], merge_w.at[y, :, xh], at(y, z, other), j)

    def y_spread(whole):
        return [push(whole.at[y], whole.at[y], at(y_by(d), z, xh), j) for d in (1, -1)]

    arrive([split_x])
    split_y = y_spread(split_w)

    half_q = lax.broadcasted_iota(jnp.int32, (ROWS, 1), 0) // (2 * QUAD)
    half_k = lax.broadcasted_iota(jnp.int32, (1, ROWS), 1) // (2 * QUAD)
    allowed = jnp.logical_or(half_q == half_k, i != lat_size - 1)
    first = lax.broadcasted_iota(jnp.int32, (ROWS, HD2), 1) < HD2 // 2
    inv_root = (HD2 // 2) ** -0.5

    def of_head(values, h):
        return jnp.where(first if h % 2 == 0 else jnp.logical_not(first), values, jnp.zeros_like(values))

    def attend(pair):
        at_q = slice(HD2 * pair, HD2 * (pair + 1))
        at_k = slice(D + HD2 * pair, D + HD2 * (pair + 1))
        at_v = slice(2 * D + HD2 * pair, 2 * D + HD2 * (pair + 1))
        q, k, v = proj[:, at_q], proj[:, at_k], proj[:, at_v]
        results = []
        for h in (2 * pair, 2 * pair + 1):
            scores = dot(of_head(q, h), k, NT) * inv_root + bias[h]
            scores = jnp.where(allowed, scores, FAR)
            weights = jnp.exp(scores - jnp.max(scores, axis=-1, keepdims=True))
            weights = weights / jnp.sum(weights, axis=-1, keepdims=True)
            att[h] = weights
            results.append(dot(weights.astype(BF16), v))
        return jnp.where(first, results[0], results[1]).astype(BF16)

    attended = [attend(0), attend(1)]

    arrive([merge_x])
    merge_y = y_spread(merge_w)
    cot_move = gather_start(cot_all)

    attended += [attend(2), attend(3)]
    attended = jnp.concatenate(attended, axis=1)
    ready(outer)
    y_rolled = (rolled + dot(attended, outer[...])).astype(BF16)
    y_out[...] = y_rolled.reshape(4, QUAD, D)
    y_in[3] = y_out[0]
    y_move = roll_out(y_out, y_in)

    row = lax.broadcasted_iota(jnp.int32, (D, D), 0)
    col = lax.broadcasted_iota(jnp.int32, (1, D), 1)
    block = col // (4 * Z)
    want = ((block // XH) * Z + (col // 4) % Z) * (4 * XH) + (block % XH) * 4 + col % 4
    swap = (row == want).astype(F32).astype(BF16)
    ready(dense)
    toks = dot(dense[...], normed[...]).astype(BF16)
    toks_all[j] = dot(toks, swap).astype(BF16)


    def y_forward(whole, halves):
        return [
            push(halves(whole, y_by(-1), 0), halves(whole, y_by(-1), 0), at(y_by(1), z, xh), j),
            push(halves(whole, y_by(1), 1), halves(whole, y_by(1), 1), at(y_by(-1), z, xh), j),
        ]

    arrive(split_y)
    split_f = y_forward(split_w, lambda w, yy, part: w.at[yy, part])
    cot_rest = gather_relay(cot_all, cot_move)

    arrive(y_move)
    ready(pair_of_quarter, merge_gain)
    y_pairs = lanes(dot(pair_of_quarter[...], y_in[...].reshape(ROWS, D)))
    pair_unit, pair_scale = norm_parts(y_pairs)
    norm_all[j] = (pair_unit * merge_gain[...]).astype(BF16)
    norm_move = gather_start(norm_all)
    toks_move = gather_start(toks_all)

    arrive(merge_y)
    merge_f = y_forward(merge_w, lambda w, yy, part: w.at[yy, pl.ds(part * (Z // 2), Z // 2)])

    arrive(cot_rest)
    arrive(split_f)

    def split_block(k):
        return split_w[:, :, k].reshape(MS, MS)

    cots = cot_all[...].reshape(lon_size * QUAD, 4 * D)
    grad_merged = dot(cots[:, :MS], split_block(0), NT)
    for k in range(1, KB):
        grad_merged = grad_merged + dot(cots[:, MS * k : MS * (k + 1)], split_block(k), NT)
    grad_merged = grad_merged.astype(BF16)
    near = (0, 1, -1, 2)

    def gm_part(first, count):
        for k in range(first, first + count):
            block = merge_w[y_by(near[k])].reshape(D, MS)
            gm_out[:, k] = dot(grad_merged, block, NT).astype(BF16).reshape(lon_size, QUAD, D)
        part = pl.ds(first, count)
        there = push(gm_out.at[beyond, part], gm_mid.at[1, part], i, mate)
        here = push(gm_out.at[mate, part], gm_mid.at[0, part], i, mate)
        arrive([there])
        pair = gm_out[across, part].astype(F32) + gm_mid[1, part].astype(F32)
        gm_far_out[part] = pair.astype(BF16)
        return [here, push(gm_far_out.at[part], gm_far_in.at[part], i, across)]

    gm_moves = gm_part(0, 3)
    arrive(merge_f)
    gm_moves += gm_part(3, 1)
    merge_full = merge_w[...].reshape(4 * D, MS)
    norm_rest = gather_relay(norm_all, norm_move)
    toks_rest = gather_relay(toks_all, toks_move)

    arrive(gm_moves)
    for k in range(4):
        found = gm_out[j, k].astype(F32) + gm_mid[0, k].astype(F32) + gm_far_in[k].astype(F32)
        gm_sum[y_by(near[k])] = found
    grad_mnorm = jnp.concatenate([gm_sum[k] for k in range(4)], axis=1)
    grad_y = cot_all[j].astype(F32) + norm_back(pair_unit, pair_scale, grad_mnorm, merge_gain[...])
    grad_y = dot(pair_of_quarter[...], stacked(grad_y.astype(BF16)), TN).astype(BF16)
    gy_out[...] = grad_y.reshape(4, QUAD, D)
    gy_in[0] = gy_out[3]
    gy_move = roll_in(gy_out, gy_in)

    arrive(norm_rest)
    merged = dot(norm_all[...].reshape(lon_size * QUAD, 4 * D), merge_full).astype(BF16)
    for k in range(KB):
        part = dot(merged, split_block(k)).astype(BF16)
        so_out[:, :, MS * k : MS * (k + 1)] = part.reshape(lon_size, QUAD, MS)
    so_start = reduce_start(so_out, so_mid)

    so_crossed = reduce_cross(so_out, so_mid, so_start, 1)
    arrive(gy_move)
    grad_rolled_y = gy_in[...].reshape(ROWS, D)
    grad_attended = dot(grad_rolled_y, outer[...], NT).astype(BF16)
    for pair in range(HEADS // 2):
        at_q = slice(HD2 * pair, HD2 * (pair + 1))
        at_k = slice(D + HD2 * pair, D + HD2 * (pair + 1))
        at_v = slice(2 * D + HD2 * pair, 2 * D + HD2 * (pair + 1))
        q, k, v = proj[:, at_q], proj[:, at_k], proj[:, at_v]
        g = grad_attended[:, at_q]
        found = []
        for h in (2 * pair, 2 * pair + 1):
            weights = att[h]
            grad_p = dot(of_head(g, h), v, NT)
            grad_v = dot(weights.astype(BF16), g, TN)
            shared = jnp.sum(weights * grad_p, axis=-1, keepdims=True)
            grad_s = (weights * (grad_p - shared)).astype(BF16)
            found.append((dot(grad_s, k) * inv_root, dot(grad_s, q, TN) * inv_root, grad_v))
        for where, even, odd in zip((at_q, at_k, at_v), *found):
            gp[:, where] = jnp.where(first, even, odd).astype(BF16)
    few = dot(dense[...], gp[...]).astype(BF16)
    for d in range(lon_size):
        gp_out[d] = few[:, CW * d : CW * (d + 1)]
    gp_far = push(gp_out.at[beyond], gp_mid, i, across)
    gp_move = [
        push(gp_out.at[across], gp_in.at[j], i, across),
        push(gp_out.at[mate], gp_in.at[j], i, mate),
    ]
    gp_in[j] = gp_out[j]

    grad_normed = dot(gp[...], inner[...], NT)
    grad_in = grad_rolled_y.astype(F32) + norm_back(unit_keep[...], scale, grad_normed, gain[...])
    gf_out[...] = grad_in.astype(BF16).reshape(4, QUAD, D)
    gf_in[3] = gf_out[0]
    gf_move = roll_out(gf_out, gf_in)

    arrive([gp_far])
    gp_move.append(push(gp_mid, gp_in.at[across], i, mate))

    arrive(toks_rest)
    arrive(gp_move[:2])
    summed = dot(toks_all[j], gp_in[j], TN) + dot(toks_all[mate], gp_in[mate], TN)
    summed = summed + dot(toks_all[across], gp_in[across], TN)
    arrive(gp_move[2:])
    summed = summed + dot(toks_all[beyond], gp_in[beyond], TN)
    dw_out[...] = summed.astype(BF16).reshape(Y * XH, 4 * Z, CW)
    dw_move = []
    for dy, dx in sorted(plane, key=lambda p: -min(p[0], Y - p[0]) - 2 * p[1]):
        yy, xx = y_by(dy), lax.rem(xh + dx, XH)
        dw_move.append(push(dw_out.at[yy * XH + xx], dw_in.at[y * XH + xh], at(yy, z, xx), j))

    def from_pairs(wide):
        return dot(to_pair[...], stacked(wide), TN).astype(BF16)

    def put(dst, rows):
        for r in range(WIN_LAT):
            for c in range(WIN_LON):
                start = (r * WIN_LON + c) * LEVELS
                dst[r, c] = rows[start : start + LEVELS]

    arrive(dw_move)
    mine = dw_out[y * XH + xh].astype(F32)
    for dy, dx in plane:
        slot = y_by(-dy) * XH + lax.rem(xh + dx, XH)
        mine = mine + dw_in[slot].astype(F32)
    mine = mine.astype(BF16)
    CB = CW // 3
    tall = jnp.concatenate([mine[:, CB * c : CB * (c + 1)] for c in range(3)], axis=0)
    row = lax.broadcasted_iota(jnp.int32, (16 * Z, 1), 0)
    col = lax.broadcasted_iota(jnp.int32, (16 * Z, 12 * Z), 1)
    inner_row = row % 16
    want = (inner_row // 4) * (4 * Z) + (row // 16) * 4 + inner_row % 4
    spread = jnp.logical_and(col == want, inner_row < 12).astype(F32).astype(BF16)
    z_out[...] = dot(spread, tall).astype(BF16).reshape(Z, 16, CB)

    for d in Z_FAR_FIRST:
        sums_z(d).start()
    z_in[z] = z_out[z]

    split_out = reduce_end(so_out, so_mid, so_crossed, 1)
    put(outputs, from_pairs((y_pairs + split_out).astype(BF16)))
    stores = [pltpu.make_async_copy(outputs, outputs_hbm, osem.at[0])]
    stores[0].start()

    arrive(gf_move)
    put(grad_fields, dot(to_quarter[...], gf_in[...].reshape(ROWS, D), TN).astype(BF16))
    stores.append(pltpu.make_async_copy(grad_fields, grad_fields_hbm, osem.at[1]))
    stores[1].start()

    @pl.loop(1, Z)
    def _(d):
        sums_z(d).wait_recv()

    owned = jnp.sum(z_in[...].astype(F32), axis=0)
    shrink = 1.0 / math.sqrt(WIN * lat_size * lon_size)
    for c in range(3):
        grad_inner[:, CB * c : CB * (c + 1)] = owned[4 * c : 4 * c + 4] * shrink

    for store in stores:
        store.wait()
    for copy in sent:
        copy.wait_send()

    @pl.loop(1, Z)
    def _(d):
        sums_z(d).wait_send()

    for kind, slot in enumerate((raw_slot, merge_slot)):
        z_wait(kind, slot, range(1, Z), received=False)


def settle_kernel(*refs):
    sources, targets, held, sems = refs[:3], refs[3:6], refs[6:9], refs[9]
    loads = [pltpu.make_async_copy(a, b, sems.at[0, k]) for k, (a, b) in enumerate(zip(sources, held))]
    stores = [pltpu.make_async_copy(a, b, sems.at[1, k]) for k, (a, b) in enumerate(zip(held, targets))]
    for load in loads:
        load.start()
    for load, store in zip(loads, stores):
        load.wait()
        store.start()
    for store in stores:
        store.wait()


def local(
    lon_size, fields, cotangent, norm_gain, inner_weight, outer_weight, bias_table, merge_gain,
    merge_weight, split_weight,
):
    D = fields.shape[-1]
    to_quarter, to_pair, pair_of_quarter, dense, pick = (jnp.asarray(a) for a in orders())
    vmem = pl.BlockSpec(memory_space=pltpu.VMEM)
    hbm = pl.BlockSpec(memory_space=pltpu.HBM)
    operands = (
        split_weight, merge_weight, fields.transpose(1, 2, 0, 3), to_quarter,
        cotangent.transpose(1, 2, 0, 3), to_pair, norm_gain.reshape(1, D), inner_weight, bias_table,
        pick, outer_weight, pair_of_quarter, merge_gain.reshape(1, 4 * D), dense,
    )
    MS, CW = D // 2, 3 * D // lon_size

    def buf(*shape, dtype=BF16):
        return pltpu.VMEM(shape, dtype)

    quarters = (4, QUAD, D)
    wide = (lon_size, QUAD, 4 * D)
    scratch = [
        buf(WIN, D), buf(*quarters), buf(*quarters), buf(*wide), buf(*wide),
        buf(Z, 16, MS), buf(64, MS, dtype=F32), buf(Y, XH, 8, 2 * Z, MS),
        buf(Y, Z, XH, 16, MS),
        buf(*quarters), buf(*quarters), buf(lon_size, 4, QUAD, D), buf(*quarters), buf(*quarters),
        buf(*quarters), buf(*quarters), buf(HEADS, ROWS, ROWS, dtype=F32), buf(ROWS, 3 * D),
        buf(ROWS, D),
        buf(lon_size, WIN, D), buf(ROWS, 3 * D), buf(lon_size, WIN, CW), buf(lon_size, WIN, CW),
        buf(Y * XH, 4 * Z, CW), buf(Y * XH, 4 * Z, CW), buf(Z, 16, CW // 3), buf(Z, 16, CW // 3),
        buf(*wide), buf(ROWS, D, dtype=F32), buf(HEADS, ROWS, ROWS, dtype=F32),
        buf(HEADS, 2 * SPAN, dtype=F32), buf(WIN, CW),
        buf(2, 4, QUAD, D), buf(4, QUAD, D), buf(4, QUAD, D), buf(4, QUAD, D, dtype=F32),
        buf(2, QUAD, 4 * D), buf(2, QUAD, 4 * D), buf(2, QUAD, 4 * D),
    ]
    count = 64
    scratch += [
        pltpu.SemaphoreType.DMA((count,)), pltpu.SemaphoreType.DMA((count,)),
        pltpu.SemaphoreType.DMA((3, Z)), pltpu.SemaphoreType.DMA((3, Z)),
        pltpu.SemaphoreType.DMA((len(operands),)),
        buf(WIN_LAT, WIN_LON, LEVELS, D), buf(WIN_LAT, WIN_LON, LEVELS, D),
        pltpu.SemaphoreType.DMA((2,)),
    ]
    scratch += [pltpu.VMEM(x.shape, x.dtype) for x in operands]
    grid_shape = (WIN_LAT, WIN_LON, LEVELS, D)
    out, grad, sums = pl.pallas_call(
        functools.partial(main_kernel, lon_size),
        out_shape=(
            jax.ShapeDtypeStruct(grid_shape, BF16),
            jax.ShapeDtypeStruct(grid_shape, BF16),
            jax.ShapeDtypeStruct((4, CW), F32),
        ),
        in_specs=[hbm] * len(operands),
        out_specs=(hbm, hbm, vmem),
        scratch_shapes=scratch,
        compiler_params=pltpu.CompilerParams(
            collective_id=0, has_side_effects=True, vmem_limit_bytes=63 * 1024 * 1024
        ),
    )(
        *operands,
    )
    results = (out, grad, sums)
    out, grad, sums = pl.pallas_call(
        settle_kernel,
        out_shape=tuple(jax.ShapeDtypeStruct(x.shape, x.dtype) for x in results),
        in_specs=[hbm] * 3,
        out_specs=(hbm,) * 3,
        scratch_shapes=[
            *(pltpu.VMEM(x.shape, x.dtype) for x in results),
            pltpu.SemaphoreType.DMA((2, 3)),
        ],
        compiler_params=pltpu.CompilerParams(vmem_limit_bytes=63 * 1024 * 1024),
    )(*results)
    return out.transpose(2, 0, 1, 3), grad.transpose(2, 0, 1, 3), sums


def solution(mesh):
    return jax.shard_map(
        functools.partial(local, mesh.shape["lon"]),
        mesh=mesh,
        in_specs=(
            P(None, "lat", "lon", None),
            P(None, "lat", "lon", None),
            P(),
            P(),
            P(),
            P(),
            P(),
            P("lat", None),
            P("lat", None),
        ),
        out_specs=(P(None, "lat", "lon", None), P(None, "lat", "lon", None), P("lat", "lon")),
        check_vma=False,
    )
```
